256 devices in a mesh: pos: 8 (over z), ch: 32 (over x, y, core).
Axes of the slice: x: 4, y: 4, z: 8, core: 2. Of those that a mesh axis runs over, the one named last changes fastest.
Arguments:
- queries: bfloat16 [8192, 4096], P('pos', 'ch'), may hold values from -6 to 6
- keys: bfloat16 [8192, 4096], P('pos', 'ch'), may hold values from -6 to 6
- values: bfloat16 [8192, 4096], P('pos', 'ch'), may hold values from -6 to 6
- residue: float32 [4096, 16], P('ch'), may hold values from -0.125 to 0.125
- rate: float32 [4096, 16], P('ch'), may hold values from 6.1035156e-05 to 0.1
- skip: float32 [4096], P('ch'), may hold values from -1 to 1
- w_out: bfloat16 [4096, 4096], P('ch'), may hold values from -0.1875 to 0.1875
- lengths: int32 [3], replicated, may hold values from 1 to 4, 8 in all
- d_out: bfloat16 [8192, 4096], P('pos', 'ch'), may hold values from -6 to 6
Outputs:
- out: bfloat16 [8192, 4096], P('pos', 'ch')
- d_queries: bfloat16 [8192, 4096], P('pos', 'ch')
- d_keys: bfloat16 [8192, 4096], P('pos', 'ch')
- d_values: bfloat16 [8192, 4096], P('pos', 'ch')
- d_residue: float32 [4096, 16], P('ch')
- d_rate: float32 [4096, 16], P('ch')
- d_skip: float32 [4096], P('ch')
- d_w_out: float32 [4096, 4096], P('ch')
The draws below stay inside these ranges and needn't reach their ends.
Inputs may be any that keep to these rules, and one draw needn't show every extreme that they name: `lengths`: lengths count whole blocks of 1024 positions and add up to 8; the longest document has exactly 4 blocks.
All inputs are finite; a program needn't handle non-finite values.
Results may differ from the reference program's by a relative error of at most 0.023.
Values may be sent and summed in bfloat16 or wider, within the bound.
A program may use at most 128 MiB of HBM per device.

```python
import math
import jax
import jax.numpy as jnp
import numpy as np
from jax import lax

D = 4096
MODES = 16
SUB = 128
TOK_DEV = 1024
NDOC = 3
TOKENS = 8192
N_POS = 8


def strengthened(result, own_key, source, target, shards_of, factor):
    def block_of(axis_at):
        return (jnp.arange(result.shape[axis_at]) // (result.shape[axis_at] // shards_of)).reshape((-1,) + (1,) * (result.ndim - 1 - axis_at))

    one_side = jax.random.permutation(own_key, shards_of)[block_of(target)]
    other_side = (block_of(target) + shards_of // 2) % shards_of
    return jnp.where((block_of(source) == one_side) | (block_of(source) == other_side), factor * result, result)


def levels(key, extent, shards, smallest, top_value):
    def one(position, shards_of):
        heights = jax.random.uniform(jax.random.fold_in(jax.random.fold_in(key, 6), position), (shards_of,), jnp.float32, smallest / len(shards), top_value / len(shards))
        return jnp.repeat(jnp.exp(heights), extent[position] // shards_of).reshape((-1,) + (1,) * (len(extent) - position - 1))

    gain = one(*shards[0])
    for cut in shards[1:]:
        gain = gain * one(*cut)
    return gain


def split_up(number_of, total, most, slope):
    portions = [(1 << 20) // math.isqrt(rank ** slope) + 1 for rank in range(2, number_of + 1)]
    surplus, counts = total - most - (number_of - 1), [1] * (number_of - 1)
    while surplus > 0:
        candidates = [i for i in range(number_of - 1) if counts[i] < most]
        mass, remaining = sum([portions[i] for i in candidates]), surplus
        for i in candidates:
            addition = min(most - counts[i], max(1, remaining * portions[i] // mass), surplus)
            counts[i] = counts[i] + addition
            surplus = surplus - addition
    return np.array([most] + counts)


def uneven(rng, count, total, reach, lean):
    if count == 2:
        one = jax.random.randint(rng, (), max(1, total - reach), min(reach, total - 1) + 1)
        return jnp.stack([one, total - one])
    sizes = jnp.asarray(split_up(count, total, reach, lean), jnp.int32)
    couples = (count - 1) // 2
    donor, sink = sizes[1:1 + 2 * couples:2], sizes[2:2 + 2 * couples:2]
    room = jnp.minimum(donor - 1, reach - sink)
    passed = jax.random.randint(jax.random.fold_in(rng, 1), (couples,), 0, 1 << 20) % (room + 1)
    sizes = sizes.at[1:1 + 2 * couples:2].set(donor - passed).at[2:2 + 2 * couples:2].set(sink + passed)
    return sizes[jax.random.permutation(jax.random.fold_in(rng, 2), count)]


def normal_values(own_key, dims, spread, bound, shards=(), kind=jnp.bfloat16):
    entries = jax.random.normal(own_key, dims, jnp.float32) * spread
    if len(shards) > 0:
        entries = levels(own_key, dims, shards, -0.22, 0.18) * entries
    return jnp.clip(entries, min=-bound, max=bound).astype(kind)


def gaussian_with(stream_key, dims, scale, limit, split, heavy, kind=jnp.bfloat16):
    entries = scale * jax.random.normal(stream_key, dims, jnp.float32)
    if split:
        entries = entries * levels(stream_key, dims, split, -0.22, 0.18)
    return jnp.clip(strengthened(entries, jax.random.fold_in(stream_key, 3), *heavy), -limit, limit).astype(kind)


def setup_inputs(seed: int = 0) -> dict:
    seeds = jax.random.split(jax.random.key(seed), 10)
    return {
        "queries": normal_values(seeds[0], (TOKENS, D), 1.0, 6.0, ((0, 8), (1, 32))),
        "keys": normal_values(seeds[1], (TOKENS, D), 1.0, 6.0, ((0, 8), (1, 32))),
        "values": normal_values(seeds[2], (TOKENS, D), 1.0, 6.0, ((0, 8), (1, 32))),
        "residue": normal_values(seeds[3], (D, MODES), ((MODES * TOK_DEV) ** -0.5), 0.125, ((0, 32),), jnp.float32),
        "rate": jnp.clip(jnp.exp(math.log(0.1) - 7.4014754 * jax.random.uniform(seeds[4], (D, MODES), jnp.float32) ** levels(seeds[4], (D, MODES), ((0, 32),), -0.2, 0.2)), 6.103515625e-05, 0.1),
        "skip": jnp.clip(jax.random.uniform(seeds[5], (D,), jnp.float32, -1.0, 1.0) * levels(seeds[5], (D,), ((0, 32),), -0.4, 0.0), -1.0, 1.0),
        "w_out": gaussian_with(seeds[6], (D, D), D ** -0.5, 0.1875, ((0, 32),), (0, 1, 32, 2.75)),
        "lengths": uneven(seeds[7], NDOC, N_POS, N_POS // 2, 0).astype(jnp.int32),
        "d_out": normal_values(seeds[8], (TOKENS, D), 1.0, 6.0, ((0, 8), (1, 32))),
    }


highest = lax.Precision.HIGHEST

def long_conv(mixed_in, residue, rate, keep_flag):
    pieces = mixed_in.shape[0] // SUB
    blocks = mixed_in.reshape(pieces, SUB, mixed_in.shape[1])
    lag_steps = jnp.arange(SUB).astype(jnp.float32)
    powers = jnp.exp(-rate[:, :, None] * lag_steps[None, None, :])
    kernel = jnp.einsum('dm,dmj->dj', residue, powers, precision=highest)
    lag_grid = jnp.arange(SUB)[:, None] - jnp.arange(SUB)[None, :]
    toeplitz = jnp.where(lag_grid[None] >= 0, jnp.take(kernel, jnp.clip(lag_grid, 0, SUB - 1), axis=1), 0.0)
    intra_part = jnp.einsum('dts,nsd->ntd', toeplitz, blocks, precision=highest)
    tail_decay = jnp.exp(-rate[:, :, None] * (SUB - lag_steps)[None, None, :])
    end_states = jnp.einsum('dms,nsd->nmd', tail_decay, blocks, precision=highest)
    sub_decay = jnp.exp(-rate * SUB).T

    def advance(carried, item):
        end_state, flag = item
        entering = carried * flag
        return (entering * sub_decay + end_state, entering)
    _, entering = lax.scan(advance, jnp.zeros(sub_decay.shape, jnp.float32), (end_states, keep_flag))
    head_decay = residue[:, :, None] * powers
    cross_part = jnp.einsum('dmt,nmd->ntd', head_decay, entering, precision=highest)
    return (intra_part + cross_part).reshape(mixed_in.shape)

def reference(queries, keys, values, residue, rate, skip, w_out, lengths, d_out):
    per_block = TOK_DEV // SUB
    begins = jnp.cumsum(lengths) - lengths
    block_ids = jnp.arange(N_POS).astype(jnp.int32)
    starts = jnp.any(block_ids[:, None] == begins[None, :], axis=1)
    sub_ids = jnp.arange(TOKENS // SUB).astype(jnp.int32)
    first_sub = sub_ids % per_block == 0
    keep_flag = jnp.where(first_sub & starts[sub_ids // per_block], 0.0, 1.0).astype(jnp.float32)
    query_full = queries.astype(jnp.float32)
    key_full = keys.astype(jnp.float32)
    value_full = values.astype(jnp.float32)
    mixed_in = key_full * value_full

    def conv_only(mixed, res, rat):
        return long_conv(mixed, res, rat, keep_flag)
    conv, pull_back = jax.vjp(conv_only, mixed_in, residue, rate)
    conv_field = conv + skip[None, :] * mixed_in
    product = (query_full * conv_field).astype(jnp.bfloat16)
    out = jnp.dot(product, w_out, preferred_element_type=jnp.float32).astype(jnp.bfloat16)
    d_product = jnp.dot(d_out, w_out.T, preferred_element_type=jnp.float32)
    d_w_out = jnp.dot(product.T, d_out, preferred_element_type=jnp.float32)
    d_queries = (d_product * conv_field).astype(jnp.bfloat16)
    d_field = d_product * query_full
    d_mixed, d_residue, d_rate = pull_back(d_field)
    d_skip = lax.optimization_barrier(jnp.sum(d_field * mixed_in, axis=0))
    d_mixed = d_mixed + skip[None, :] * d_field
    d_keys = (d_mixed * value_full).astype(jnp.bfloat16)
    d_values = (d_mixed * key_full).astype(jnp.bfloat16)
    return (out, d_queries, d_keys, d_values, d_residue, d_rate, d_skip, d_w_out)
```

```python
import functools

import jax
import jax.numpy as jnp
from jax import lax
from jax.experimental import pallas as pl
from jax.experimental.pallas import tpu as pltpu
from jax.sharding import PartitionSpec as P

f32 = jnp.float32
bf16 = jnp.bfloat16
MODES = 16
GROUP = 8
NSUB = 8
UNROLL = 4


def rows_of(s):
    return pl.ds(pl.multiple_of(s * NSUB, NSUB), NSUB)


def interleave(dst, val):
    sub = val.shape[0] // NSUB
    for n in range(NSUB):
        dst[pl.ds(n, sub, stride=NSUB), :] = val[n * sub : (n + 1) * sub]


def deinterleave(src):
    sub = src.shape[0] // NSUB
    return jnp.concatenate([src[pl.ds(n, sub, stride=NSUB), :] for n in range(NSUB)], axis=0)


def spread(a):
    return jnp.broadcast_to(a[:, None, :], (a.shape[0], NSUB, a.shape[1]))


def place_of(shape):
    return lax.broadcasted_iota(jnp.int32, shape, 1)


def scan_states(src, rate, reverse):
    sub = src.shape[0] // NSUB
    lam = spread(jnp.exp(-rate))

    def step(i, h):
        s = sub - 1 - i if reverse else i
        return lam * h + src[rows_of(s), :][None]

    p = lax.fori_loop(0, sub, step, jnp.zeros_like(lam), unroll=UNROLL)
    place = place_of(p.shape)
    for k in (1, 2, 4):
        moved = pltpu.roll(p, NSUB - k if reverse else k, 1)
        ok = place < NSUB - k if reverse else place >= k
        p = p + spread(jnp.exp(-rate * (sub * k))) * jnp.where(ok, moved, 0.0)
    return p


def edge_of(p, reverse):
    return jnp.sum(jnp.where(place_of(p.shape) == (0 if reverse else NSUB - 1), p, 0.0), axis=1)


def entering_of(p, rate, sub, carry, reverse):
    place = place_of(p.shape)
    moved = pltpu.roll(p, NSUB - 1 if reverse else 1, 1)
    ok = place < NSUB - 1 if reverse else place >= 1
    steps = (NSUB - 1 - place if reverse else place).astype(f32) * float(sub)
    return jnp.where(ok, moved, 0.0) + jnp.exp(-spread(rate) * steps) * spread(carry)


def forward_pass(xs, ys, hs, rate, residue, start):
    sub = xs.shape[0] // NSUB
    for lo in range(0, MODES, GROUP):
        part = slice(lo, lo + GROUP)
        lam, res = spread(jnp.exp(-rate[part])), spread(residue[part])

        def step(s, h):
            if hs is not None:
                hs[s, part] = h
            h = lam * h + xs[rows_of(s), :][None]
            if ys is not None:
                y = jnp.sum(res * h, axis=0)
                ys[rows_of(s), :] = y if lo == 0 else ys[rows_of(s), :] + y
            return h

        lax.fori_loop(0, sub, step, start[part], unroll=UNROLL)


def backward_pass(xs, gs, ms, hs, rate, residue, start):
    sub = xs.shape[0] // NSUB
    d_res, d_rate = [], []
    for lo in range(0, MODES, GROUP):
        part = slice(lo, lo + GROUP)
        lam, res = spread(jnp.exp(-rate[part])), spread(residue[part])

        def step(i, carry):
            a, dr, dt = carry
            s = sub - 1 - i
            a = lam * a + gs[rows_of(s), :][None]
            m = jnp.sum(res * a, axis=0)
            ms[rows_of(s), :] = m if lo == 0 else ms[rows_of(s), :] + m
            return a, dr + a * xs[rows_of(s), :][None], dt + a * hs[s, part]

        zero = jnp.zeros_like(lam)
        _, dr, dt = lax.fori_loop(0, sub, step, (start[part], zero, zero), unroll=UNROLL)
        d_res.append(jnp.sum(dr, axis=1))
        d_rate.append(-residue[part] * jnp.exp(-rate[part]) * jnp.sum(dt, axis=1))
    return jnp.concatenate(d_res, axis=0), jnp.concatenate(d_rate, axis=0)


def k_sum(k, v, rate, s_out, xs):
    interleave(xs, k[...].astype(f32) * v[...].astype(f32))
    s_out[...] = edge_of(scan_states(xs, rate[...], False), False)


def k_main(q, k, v, rate, residue, skip, carry, field, product, xs, ys):
    x = k[...].astype(f32) * v[...].astype(f32)
    interleave(xs, x)
    sub = xs.shape[0] // NSUB
    p = scan_states(xs, rate[...], False)
    start = entering_of(p, rate[...], sub, carry[...], False)
    forward_pass(xs, ys, None, rate[...], residue[...], start)
    c = deinterleave(ys) + skip[...] * x
    field[...] = c
    product[...] = (q[...].astype(f32) * c).astype(bf16)


def k_back_sum(q, dp, rate, a_out, gs):
    interleave(gs, dp[...] * q[...].astype(f32))
    a_out[...] = edge_of(scan_states(gs, rate[...], True), True)


def k_back(q, k, v, dp, field, rate, residue, skip, carry, later, dq, dk, dv, dres, drate, dskip, xs, gs, ms, hs):
    kk, vv = k[...].astype(f32), v[...].astype(f32)
    x = kk * vv
    g = dp[...] * q[...].astype(f32)
    interleave(xs, x)
    interleave(gs, g)
    sub = xs.shape[0] // NSUB
    r = rate[...]
    start = entering_of(scan_states(xs, r, False), r, sub, carry[...], False)
    forward_pass(xs, None, hs, r, residue[...], start)
    start = entering_of(scan_states(gs, r, True), r, sub, later[...], True)
    dres[...], drate[...] = backward_pass(xs, gs, ms, hs, r, residue[...], start)
    dskip[...] = jnp.sum(x * g, axis=0, keepdims=True)
    dq[...] = (dp[...] * field[...]).astype(bf16)
    dm = deinterleave(ms) + skip[...] * g
    dk[...] = (dm * vv).astype(bf16)
    dv[...] = (dm * kk).astype(bf16)


def call(kernel, outs, scratch, *args):
    return pl.pallas_call(
        kernel,
        out_shape=outs,
        scratch_shapes=scratch,
        compiler_params=pltpu.CompilerParams(vmem_limit_bytes=48 * 1024 * 1024),
    )(*args)


def carried(edge, rate, steps, weights, reverse):
    every = lax.all_gather(edge, "pos")
    place = lax.axis_index("pos")
    total = jnp.zeros_like(edge)
    for k in (1, 2, 3):
        other = (place + k if reverse else place - k) % every.shape[0]
        total += weights[k - 1] * jnp.exp(-rate * (steps * (k - 1))) * every[other]
    return total


def shards(queries, keys, values, residue, rate, skip, w_out, lengths, d_out):
    t, c = queries.shape
    rate, residue, skip = rate.T, residue.T, skip[None, :]
    place, count = lax.axis_index("pos"), lax.axis_size("pos")
    ends = jnp.cumsum(lengths)
    document = lambda b: jnp.sum((ends <= b).astype(jnp.int32))

    def weight(other):
        inside = (other >= 0) & (other < count)
        return jnp.where(inside & (document(other) == document(place)), 1.0, 0.0).astype(f32)

    before = [weight(place - k) for k in (1, 2, 3)]
    after = [weight(place + k) for k in (1, 2, 3)]
    state = jax.ShapeDtypeStruct((MODES, c), f32)
    wide = jax.ShapeDtypeStruct((t, c), f32)
    thin = jax.ShapeDtypeStruct((t, c), bf16)
    big = pltpu.VMEM((t, c), f32)
    edge = call(k_sum, state, [big], keys, values, rate)
    carry = carried(edge, rate, float(t), before, False)
    field, product = call(
        k_main, (wide, thin), [big, big], queries, keys, values, rate, residue, skip, carry
    )
    gathered = lax.all_gather(d_out, "ch", axis=1, tiled=True)
    dp = lax.dot_general(gathered, w_out, (((1,), (1,)), ((), ())), preferred_element_type=f32)
    edge = call(k_back_sum, state, [big], queries, dp, rate)
    later = carried(edge, rate, float(t), after, True)
    dq, dk, dv, dres, drate, dskip = call(
        k_back,
        (thin, thin, thin, state, state, jax.ShapeDtypeStruct((1, c), f32)),
        [big, big, big, pltpu.VMEM((t // NSUB, MODES, NSUB, c), f32)],
        queries, keys, values, dp, field, rate, residue, skip, carry, later,
    )
    dw = lax.dot_general(product, gathered, (((0,), (0,)), ((), ())), preferred_element_type=f32)
    dw = lax.psum(dw.astype(bf16), "pos").astype(f32)
    part = lax.dot_general(w_out, product, (((0,), (1,)), ((), ())), preferred_element_type=f32)
    out = lax.psum_scatter(part.astype(bf16), "ch", scatter_dimension=0, tiled=True).T
    small = lax.psum(jnp.concatenate([dres, drate, dskip], axis=0).astype(bf16), "pos").astype(f32)
    return out, dq, dk, dv, small[:MODES].T, small[MODES : 2 * MODES].T, small[2 * MODES], dw


def solution(mesh):
    both, chan = P("pos", "ch"), P("ch", None)
    return jax.shard_map(
        shards,
        mesh=mesh,
        in_specs=(both, both, both, chan, chan, P("ch"), chan, P(), both),
        out_specs=(both, both, both, both, chan, chan, P("ch"), chan),
        check_vma=False,
    )
```

```python
import functools

import jax
import jax.numpy as jnp
from jax import lax
from jax.experimental import pallas as pl
from jax.experimental.pallas import tpu as pltpu
from jax.sharding import PartitionSpec as P

f32 = jnp.float32
bf16 = jnp.bfloat16
MODES = 16
GROUP = 8
NSUB = 8
UNROLL = 4
SIDE = 4
CHIPS = SIDE * SIDE
STREAMS = 4
MESH = pl.DeviceIdType.MESH
MIB = 1024 * 1024


def rows_of(s):
    return pl.ds(pl.multiple_of(s * NSUB, NSUB), NSUB)


def interleave(dst, val):
    sub = val.shape[0] // NSUB
    for n in range(NSUB):
        dst[pl.ds(n, sub, stride=NSUB), :] = val[n * sub : (n + 1) * sub]


def deinterleave(src):
    sub = src.shape[0] // NSUB
    return jnp.concatenate([src[pl.ds(n, sub, stride=NSUB), :] for n in range(NSUB)], axis=0)


def spread(a):
    return jnp.broadcast_to(a[:, None, :], (a.shape[0], NSUB, a.shape[1]))


def place_of(shape):
    return lax.broadcasted_iota(jnp.int32, shape, 1)


def scan_states(src, rate, reverse):
    sub = src.shape[0] // NSUB
    lam = spread(jnp.exp(-rate))

    def step(i, h):
        s = sub - 1 - i if reverse else i
        return lam * h + src[rows_of(s), :][None]

    p = lax.fori_loop(0, sub, step, jnp.zeros_like(lam), unroll=UNROLL)
    place = place_of(p.shape)
    for k in (1, 2, 4):
        moved = pltpu.roll(p, NSUB - k if reverse else k, 1)
        ok = place < NSUB - k if reverse else place >= k
        p = p + spread(jnp.exp(-rate * (sub * k))) * jnp.where(ok, moved, 0.0)
    return p


def edge_of(p, reverse):
    return jnp.sum(jnp.where(place_of(p.shape) == (0 if reverse else NSUB - 1), p, 0.0), axis=1)


def entering_of(p, rate, sub, carry, reverse):
    place = place_of(p.shape)
    moved = pltpu.roll(p, NSUB - 1 if reverse else 1, 1)
    ok = place < NSUB - 1 if reverse else place >= 1
    steps = (NSUB - 1 - place if reverse else place).astype(f32) * float(sub)
    return jnp.where(ok, moved, 0.0) + jnp.exp(-spread(rate) * steps) * spread(carry)


def forward_pass(xs, ys, hs, rate, residue, start):
    sub = xs.shape[0] // NSUB
    for lo in range(0, MODES, GROUP):
        part = slice(lo, lo + GROUP)
        lam, res = spread(jnp.exp(-rate[part])), spread(residue[part])

        def step(s, h):
            hs[s, part] = h
            h = lam * h + xs[rows_of(s), :][None]
            y = jnp.sum(res * h, axis=0)
            ys[rows_of(s), :] = y if lo == 0 else ys[rows_of(s), :] + y
            return h

        lax.fori_loop(0, sub, step, start[part], unroll=UNROLL)


def backward_pieces(xs, gs, ms, hs, rate, residue, start, pieces, result):
    sub = xs.shape[0] // NSUB
    span = sub // pieces
    d_res, d_rate = [], []
    for lo in range(0, MODES, GROUP):
        part = slice(lo, lo + GROUP)
        lam, res = spread(jnp.exp(-rate[part])), spread(residue[part])

        def step(i, carry):
            a, dr, dt = carry
            s = sub - 1 - i
            a = lam * a + gs[rows_of(s), :][None]
            m = jnp.sum(res * a, axis=0)
            ms[rows_of(s), :] = m if lo == 0 else ms[rows_of(s), :] + m
            return a, dr + a * xs[rows_of(s), :][None], dt + a * hs[s, part]

        zero = jnp.zeros_like(lam)
        carry = (start[part], zero, zero)
        for piece in range(pieces):
            carry = lax.fori_loop(piece * span, (piece + 1) * span, step, carry, unroll=UNROLL)
            yield
        d_res.append(jnp.sum(carry[1], axis=1))
        d_rate.append(-residue[part] * jnp.exp(-rate[part]) * jnp.sum(carry[2], axis=1))
    result.extend(d_res + d_rate)


class Links:
    def __init__(self):
        self.sent = []

    def copy(self, src, dst, send, recv, device):
        return pltpu.make_async_remote_copy(
            src_ref=src, dst_ref=dst, send_sem=send, recv_sem=recv,
            device_id=device, device_id_type=MESH,
        )

    def send(self, *args):
        c = self.copy(*args)
        c.start()
        self.sent.append(c)

    def drain(self):
        for c in self.sent:
            c.wait_send()
        self.sent = []


class Gather:
    def __init__(self, links, buf, send, recv, z, x, y, core):
        self.links, self.buf, self.send_sem, self.recv_sem = links, buf, send, recv
        self.z, self.at, self.core = z, (x, y), core

    def axes(self, s):
        return (0, 1, 1 - 2 * (s % 2)) if s < 2 else (1, 0, 1 - 2 * (s % 2))

    def region(self, s, i, j):
        a, b, sign = self.axes(s)
        at = list(self.at)
        at[a] = lax.rem(at[a] - sign * i + SIDE, SIDE)
        at[b] = lax.rem(at[b] - sign * j + SIDE, SIDE)
        chip = at[0] * SIDE + at[1]
        rows = self.buf.shape[0] // STREAMS
        wide = self.buf.shape[1] // CHIPS
        return self.buf.at[pl.ds(s * rows, rows), pl.ds(pl.multiple_of(chip * wide, wide), wide)]

    def device(self, s, second):
        sign = self.axes(s)[2]
        axis = self.axes(s)[1 if second else 0]
        at = list(self.at)
        at[axis] = lax.rem(at[axis] + sign + SIDE, SIDE)
        return (self.z, (at[0] * SIDE + at[1]) * 2 + self.core)

    def copy(self, s, i, j, second):
        here = self.region(s, i, j)
        k = i * SIDE + j
        return (
            here, here, self.send_sem.at[s, k, second],
            self.recv_sem.at[s, k + (1 if second else SIDE)], self.device(s, second),
        )

    def wave(self, k):
        for i in range(min(k, SIDE - 1), -1, -1):
            j = k - i
            if j >= SIDE:
                continue
            for s in range(STREAMS):
                if k > 0:
                    second = 1 if j else 0
                    came = self.copy(s, i - (1 - second), j - second, second)
                    here = self.region(s, i, j)
                    self.links.copy(here, here, came[2], came[3], came[4]).wait_recv()
                if j == 0 and i < SIDE - 1:
                    self.links.send(*self.copy(s, i, j, 0))
                if j < SIDE - 1:
                    self.links.send(*self.copy(s, i, j, 1))


def lanes(i, width):
    return pl.ds(pl.multiple_of(i * width, width), width)


def kernel(
    count, q, key, val, w, d_out, rate_ref, res_ref, skip, weights,
    out, dq, dk, dv, small, dw,
    G, H, W2, WC, xs, gs, ys, hs, field, dp, dp_send, prod, out_send, out_all,
    states, state_got, small_all, dw_own, dw_send, dw_got, ring, dw_all,
    g_send, g_recv, h_send, h_recv, loc, one_s, one_r, a2a_s, a2a_r, wz_s, wz_r,
    st_s, st_r, sm_s, sm_r, rs_s, rs_r, ag_s, ag_r,
):
    z, ch = lax.axis_index("pos"), lax.axis_index("ch")
    core, chip = lax.rem(ch, 2), lax.div(ch, 2)
    x, y = lax.div(chip, SIDE), lax.rem(chip, SIDE)
    mate = (z, chip * 2 + 1 - core)
    other = 1 - core
    t, c = q.shape
    half = t // 2
    wide = 2 * c
    n_out = w.shape[1]

    def along(k):
        return (lax.rem(z + k + count, count), ch)

    def chip_at(k):
        return lax.rem(chip + k, CHIPS)

    barrier = pltpu.get_barrier_semaphore()
    peers = [mate] + [along(k) for k in range(1, count)]
    peers += [(z, chip_at(k) * 2 + core) for k in range(1, CHIPS)]
    for device in peers:
        pl.semaphore_signal(barrier, inc=1, device_id=device, device_id_type=MESH)

    mine, its = lanes(core, half), lanes(other, half)
    own_cols = pl.ds(pl.multiple_of(chip * wide + core * c, c), c)
    mate_cols = pl.ds(pl.multiple_of(chip * wide + other * c, c), c)
    slab = c // count
    own_rows = pl.ds(pl.multiple_of(z * slab, slab), slab)
    slab_rows = pl.ds(pl.multiple_of(core * c + z * slab, slab), slab)
    local = [
        pltpu.make_async_copy(d_out.at[mine], G.at[:, own_cols], loc.at[0]),
        pltpu.make_async_copy(w, W2.at[lanes(core, c)], loc.at[1]),
        pltpu.make_async_copy(
            w.at[own_rows, lanes(chip, wide)], WC.at[chip, slab_rows], loc.at[2]
        ),
    ]
    for copy in local:
        copy.start()
    pl.semaphore_wait(barrier, len(peers))

    links = Links()
    links.send(d_out.at[its], G.at[:, own_cols], one_s.at[0], one_r.at[0], mate)
    for k in range(1, CHIPS):
        links.send(
            w.at[own_rows, lanes(chip_at(k), wide)], WC.at[chip, slab_rows],
            a2a_s.at[k], a2a_r.at[k], (z, chip_at(k) * 2 + core),
        )

    def got_one(ref, i):
        links.copy(ref, ref, one_s.at[i], one_r.at[i], mate).wait_recv()

    rate, residue = rate_ref[...], res_ref[...]
    xx = key[...].astype(f32) * val[...].astype(f32)
    interleave(xs, xx)
    local[0].wait()
    got_one(G.at[:, mate_cols], 0)
    first = Gather(links, G, g_send, g_recv, z, x, y, core)
    first.wave(0)
    sub = t // NSUB
    p = scan_states(xs, rate, False)
    states[0] = edge_of(p, False)
    for n in (1, 2, 3):
        links.send(
            states.at[0], state_got.at[0, n - 1], st_s.at[0, n - 1], st_r.at[0, n - 1], along(n)
        )
    local[1].wait()
    links.send(w, W2.at[lanes(core, c)], one_s.at[1], one_r.at[1], mate)
    first.wave(1)

    def carried(way):
        total = None
        for n in (1, 2, 3):
            here = state_got.at[way, n - 1]
            links.copy(here, here, st_s.at[way, n - 1], st_r.at[way, n - 1], mate).wait_recv()
            row = 3 * way + n - 1
            term = weights[row : row + 1, :] * jnp.exp(-rate * float(t * (n - 1))) * here[...]
            total = term if total is None else total + term
        return total

    start = entering_of(p, rate, sub, carried(0), False)
    forward_pass(xs, ys, hs, rate, residue, start)
    first.wave(2)
    cc = deinterleave(ys) + skip[...] * xx
    field[...] = cc
    prod[...] = (q[...].astype(f32) * cc).astype(bf16)
    links.send(prod.at[its], H.at[:, own_cols], one_s.at[2], one_r.at[2], mate)
    H[:, own_cols] = prod[mine, :]
    first.wave(3)
    local[2].wait()
    for k in range(1, CHIPS):
        here = WC.at[chip_at(CHIPS - k), slab_rows]
        links.copy(here, here, a2a_s.at[k], a2a_r.at[k], mate).wait_recv()
    for n in range(1, count):
        links.send(
            WC.at[:, slab_rows], WC.at[:, slab_rows], wz_s.at[n], wz_r.at[n], along(n)
        )
    got_one(H.at[:, mate_cols], 2)
    second = Gather(links, H, h_send, h_recv, z, x, y, core)
    first.wave(4)
    second.wave(0)
    first.wave(5)
    second.wave(1)
    first.wave(6)
    second.wave(2)

    got_one(W2.at[lanes(other, c)], 1)
    deep = n_out // 4
    acc = None
    for j in range(4):
        cols = pl.ds(j * deep, deep)
        term = lax.dot_general(
            G[:, cols], W2[:, cols], (((1,), (1,)), ((), ())), preferred_element_type=f32
        )
        acc = term if acc is None else acc + term
    is_first = core == 0
    dp[mine, :] = jnp.where(is_first, acc[:, :c], acc[:, c:])
    dp_send[...] = jnp.where(is_first, acc[:, c:], acc[:, :c])
    links.send(dp_send, dp.at[mine], one_s.at[3], one_r.at[3], mate)

    mate_t = H[:, mate_cols].T
    own_t = H[:, own_cols].T
    both = jnp.concatenate([mate_t, own_t], axis=0)
    block = n_out // 8
    for j in range(8):
        cols = pl.ds(j * block, block)
        r = jnp.dot(both, G[:, cols], preferred_element_type=f32)
        dw_send[:, cols] = r[:c].astype(bf16)
        dw_own[:, cols] = r[c:]
    links.send(dw_send, dw_got, one_s.at[4], one_r.at[4], mate)

    got_one(dp.at[its], 3)
    g = dp[...] * q[...].astype(f32)
    interleave(gs, g)
    p = scan_states(gs, rate, True)
    states[1] = edge_of(p, True)
    for n in (1, 2, 3):
        links.send(
            states.at[1], state_got.at[1, n - 1], st_s.at[1, n - 1], st_r.at[1, n - 1], along(-n)
        )
    second.wave(3)
    got_one(dw_got, 4)

    ways = [(way, lot) for lot in range(2) for way in range(2)]
    lot_rows = c // 2
    span = n_out // 2 // count

    def place(way, s):
        return pl.ds(pl.multiple_of(way * (n_out // 2) + s * span, span), span)

    def local_sum(way, lot, s):
        cols, rows = place(way, s), pl.ds(lot * lot_rows, lot_rows)
        return dw_own[rows, cols] + dw_got[rows, cols].astype(f32)

    def turn(way, k):
        sign = 1 - 2 * way
        return lax.rem(z + sign * k + 2 * count, count)

    def reduce_steps():
        for way, lot in ways:
            ring[way, lot, 0] = local_sum(way, lot, turn(way, -1)).astype(bf16)
        for step in range(count):
            for way, lot in ways:
                here = ring.at[way, lot, step]
                if step > 0:
                    links.copy(
                        here, here, rs_s.at[way, lot, step - 1], rs_r.at[way, lot, step - 1], mate
                    ).wait_recv()
                    s = turn(way, -1 - step)
                    total = (here[...].astype(f32) + local_sum(way, lot, s)).astype(bf16)
                    if step < count - 1:
                        here[...] = total
                    else:
                        dw_all[pl.ds(lot * lot_rows, lot_rows), place(way, s)] = total
                if step < count - 1:
                    links.send(
                        here, ring.at[way, lot, step + 1], rs_s.at[way, lot, step],
                        rs_r.at[way, lot, step], along(1 - 2 * way),
                    )
            if step < count - 1:
                yield
        for step in range(count):
            for way, lot in ways:
                here = dw_all.at[pl.ds(lot * lot_rows, lot_rows), place(way, turn(way, -step))]
                if step > 0:
                    links.copy(
                        here, here, ag_s.at[way, lot, step - 1], ag_r.at[way, lot, step - 1], mate
                    ).wait_recv()
                if step < count - 1:
                    links.send(
                        here, here, ag_s.at[way, lot, step], ag_r.at[way, lot, step],
                        along(1 - 2 * way),
                    )
            yield

    reduce = reduce_steps()
    next(reduce)
    start = entering_of(p, rate, sub, carried(1), True)
    result = []
    back = backward_pieces(xs, gs, ys, hs, rate, residue, start, 2, result)
    waves = [4, 5, 6]
    for step in range(5):
        next(back, None)
        next(reduce)
        if waves and step > 0:
            second.wave(waves.pop(0))

    dskip = jnp.sum(xx * g, axis=0, keepdims=True)
    for n in range(2):
        small_all[z, n * GROUP : (n + 1) * GROUP] = result[n]
        small_all[z, MODES + n * GROUP : MODES + (n + 1) * GROUP] = result[2 + n]
    small_all[z, 2 * MODES :] = jnp.broadcast_to(dskip, (GROUP, c))
    for n in range(1, count):
        links.send(small_all.at[z], small_all.at[z], sm_s.at[n], sm_r.at[n], along(n))
    next(reduce)
    dq[...] = (dp[...] * field[...]).astype(bf16)
    dm = deinterleave(ys) + skip[...] * g
    dk[...] = (dm * val[...].astype(f32)).astype(bf16)
    dv[...] = (dm * key[...].astype(f32)).astype(bf16)
    next(reduce)

    for n in range(1, count):
        here = WC.at[:, pl.ds(pl.multiple_of(core * c + turn(0, -n) * slab, slab), slab)]
        links.copy(here, here, wz_s.at[n], wz_r.at[n], mate).wait_recv()
    links.send(WC.at[:, lanes(core, c)], WC.at[:, lanes(core, c)], one_s.at[5], one_r.at[5], mate)
    next(reduce)
    got_one(WC.at[:, lanes(other, c)], 5)
    acc = None
    for j in range(4):
        per = CHIPS // 4
        term = jnp.dot(
            H[:, pl.ds(j * per * wide, per * wide)],
            WC[j * per : (j + 1) * per].reshape(per * wide, wide),
            preferred_element_type=f32,
        )
        acc = term if acc is None else acc + term
    out_all[mine, :] = jnp.where(is_first, acc[:, :c], acc[:, c:]).astype(bf16)
    out_send[...] = jnp.where(is_first, acc[:, c:], acc[:, :c]).astype(bf16)
    links.send(out_send, out_all.at[mine], one_s.at[6], one_r.at[6], mate)
    for _ in reduce:
        pass
    got_one(out_all.at[its], 6)
    out[...] = out_all[...]
    dw[...] = dw_all[...].astype(f32)
    for n in range(1, count):
        here = small_all.at[turn(0, -n)]
        links.copy(here, here, sm_s.at[n], sm_r.at[n], mate).wait_recv()
    total = small_all[0]
    for n in range(1, count):
        total = total + small_all[n]
    small[...] = total
    links.drain()


def shards(queries, keys, values, residue, rate, skip, w_out, lengths, d_out):
    t, c = queries.shape
    n_out = w_out.shape[1]
    place, count = lax.axis_index("pos"), lax.axis_size("pos")
    ends = jnp.cumsum(lengths)
    document = lambda b: jnp.sum((ends <= b).astype(jnp.int32))

    def weight(other):
        inside = (other >= 0) & (other < count)
        return jnp.where(inside & (document(other) == document(place)), 1.0, 0.0).astype(f32)

    weights = jnp.stack([weight(place + n) for n in (-1, -2, -3, 1, 2, 3)])
    weights = jnp.broadcast_to(weights[:, None], (6, c))
    thin = jax.ShapeDtypeStruct((t, c), bf16)
    rows = 2 * MODES + GROUP
    vmem, dma = pltpu.VMEM, pltpu.SemaphoreType.DMA
    wide, half = 2 * c, t // 2
    tall = vmem((t, c), f32)
    scratch = [
        vmem((half, n_out), bf16), vmem((half, n_out), bf16), vmem((wide, n_out), bf16),
        vmem((CHIPS, wide, wide), bf16), tall, tall, tall,
        vmem((t // NSUB, MODES, NSUB, c), f32), tall, tall, vmem((half, c), f32),
        vmem((t, c), bf16), vmem((half, c), bf16), vmem((t, c), bf16),
        vmem((2, MODES, c), f32), vmem((2, 3, MODES, c), f32), vmem((count, rows, c), f32),
        vmem((c, n_out), f32), vmem((c, n_out), bf16), vmem((c, n_out), bf16),
        vmem((2, 2, count, c // 2, n_out // 2 // count), bf16), vmem((c, n_out), bf16),
        dma((STREAMS, CHIPS, 2)), dma((STREAMS, CHIPS)), dma((STREAMS, CHIPS, 2)),
        dma((STREAMS, CHIPS)), dma((3,)), dma((7,)), dma((7,)), dma((CHIPS,)), dma((CHIPS,)),
        dma((count,)), dma((count,)), dma((2, 3)), dma((2, 3)), dma((count,)), dma((count,)),
        dma((2, 2, count)), dma((2, 2, count)), dma((2, 2, count)), dma((2, 2, count)),
    ]
    whole = pl.BlockSpec(memory_space=pltpu.VMEM)
    apart = pl.BlockSpec(memory_space=pl.ANY)
    out, dq, dk, dv, small, dw = pl.pallas_call(
        functools.partial(kernel, count),
        out_shape=(
            thin, thin, thin, thin, jax.ShapeDtypeStruct((rows, c), f32),
            jax.ShapeDtypeStruct((c, n_out), f32),
        ),
        in_specs=[whole] * 3 + [apart] * 2 + [whole] * 4,
        out_specs=(whole,) * 6,
        scratch_shapes=scratch,
        compiler_params=pltpu.CompilerParams(
            collective_id=0, has_side_effects=True, vmem_limit_bytes=60 * MIB
        ),
    )(queries, keys, values, w_out, d_out, rate.T, residue.T, skip[None, :], weights)
    return out, dq, dk, dv, small[:MODES].T, small[MODES : 2 * MODES].T, small[2 * MODES], dw


def solution(mesh):
    both, chan = P("pos", "ch"), P("ch", None)
    return jax.shard_map(
        shards,
        mesh=mesh,
        in_specs=(both, both, both, chan, chan, P("ch"), chan, P(), both),
        out_specs=(both, both, both, both, chan, chan, P("ch"), chan),
        check_vma=False,
    )
```

```python
import functools

import jax
import jax.numpy as jnp
from jax import lax
from jax.experimental import pallas as pl
from jax.experimental.pallas import tpu as pltpu
from jax.sharding import PartitionSpec as P

f32 = jnp.float32
bf16 = jnp.bfloat16
MODES = 16
GROUP = 8
NSUB = 8
UNROLL = 4
SIDE = 4
CHIPS = SIDE * SIDE
STREAMS = 4
LOTS = 4
MESH = pl.DeviceIdType.MESH
MIB = 1024 * 1024


def rows_of(s):
    return pl.ds(pl.multiple_of(s * NSUB, NSUB), NSUB)


def interleave(dst, val):
    sub = val.shape[0] // NSUB
    for n in range(NSUB):
        dst[pl.ds(n, sub, stride=NSUB), :] = val[n * sub : (n + 1) * sub]


def deinterleave(src):
    sub = src.shape[0] // NSUB
    return jnp.concatenate([src[pl.ds(n, sub, stride=NSUB), :] for n in range(NSUB)], axis=0)


def spread(a):
    return jnp.broadcast_to(a[:, None, :], (a.shape[0], NSUB, a.shape[1]))


def place_of(shape):
    return lax.broadcasted_iota(jnp.int32, shape, 1)


def scan_states(src, rate, reverse):
    sub = src.shape[0] // NSUB
    lam = spread(jnp.exp(-rate))

    def step(i, h):
        s = sub - 1 - i if reverse else i
        return lam * h + src[rows_of(s), :][None]

    p = lax.fori_loop(0, sub, step, jnp.zeros_like(lam), unroll=UNROLL)
    place = place_of(p.shape)
    for k in (1, 2, 4):
        moved = pltpu.roll(p, NSUB - k if reverse else k, 1)
        ok = place < NSUB - k if reverse else place >= k
        p = p + spread(jnp.exp(-rate * (sub * k))) * jnp.where(ok, moved, 0.0)
    return p


def edge_of(p, reverse):
    return jnp.sum(jnp.where(place_of(p.shape) == (0 if reverse else NSUB - 1), p, 0.0), axis=1)


def entering_of(p, rate, sub, carry, reverse):
    place = place_of(p.shape)
    moved = pltpu.roll(p, NSUB - 1 if reverse else 1, 1)
    ok = place < NSUB - 1 if reverse else place >= 1
    steps = (NSUB - 1 - place if reverse else place).astype(f32) * float(sub)
    return jnp.where(ok, moved, 0.0) + jnp.exp(-spread(rate) * steps) * spread(carry)


def forward_pass(xs, ys, hs, rate, residue, start):
    sub = xs.shape[0] // NSUB
    for lo in range(0, MODES, GROUP):
        part = slice(lo, lo + GROUP)
        lam, res = spread(jnp.exp(-rate[part])), spread(residue[part])

        def step(s, h):
            hs[s, part] = h
            h = lam * h + xs[rows_of(s), :][None]
            y = jnp.sum(res * h, axis=0)
            ys[rows_of(s), :] = y if lo == 0 else ys[rows_of(s), :] + y
            return h

        lax.fori_loop(0, sub, step, start[part], unroll=UNROLL)


def backward_pieces(xs, gs, ms, hs, rate, residue, start, pieces, result):
    sub = xs.shape[0] // NSUB
    span = sub // pieces
    d_res, d_rate = [], []
    for lo in range(0, MODES, GROUP):
        part = slice(lo, lo + GROUP)
        lam, res = spread(jnp.exp(-rate[part])), spread(residue[part])

        def step(i, carry):
            a, dr, dt = carry
            s = sub - 1 - i
            a = lam * a + gs[rows_of(s), :][None]
            m = jnp.sum(res * a, axis=0)
            ms[rows_of(s), :] = m if lo == 0 else ms[rows_of(s), :] + m
            return a, dr + a * xs[rows_of(s), :][None], dt + a * hs[s, part]

        zero = jnp.zeros_like(lam)
        carry = (start[part], zero, zero)
        for piece in range(pieces):
            carry = lax.fori_loop(piece * span, (piece + 1) * span, step, carry, unroll=UNROLL)
            yield
        d_res.append(jnp.sum(carry[1], axis=1))
        d_rate.append(-residue[part] * jnp.exp(-rate[part]) * jnp.sum(carry[2], axis=1))
    result.extend(d_res + d_rate)


class Links:
    def __init__(self):
        self.sent = []

    def copy(self, src, dst, send, recv, device):
        return pltpu.make_async_remote_copy(
            src_ref=src, dst_ref=dst, send_sem=send, recv_sem=recv,
            device_id=device, device_id_type=MESH,
        )

    def send(self, *args):
        c = self.copy(*args)
        c.start()
        self.sent.append(c)

    def drain(self):
        for c in self.sent:
            c.wait_send()
        self.sent = []


class Gather:
    def __init__(self, links, buf, send, recv, z, x, y, core):
        self.links, self.buf, self.send_sem, self.recv_sem = links, buf, send, recv
        self.z, self.at, self.core = z, (x, y), core

    def axes(self, s):
        return (0, 1, 1 - 2 * (s % 2)) if s < 2 else (1, 0, 1 - 2 * (s % 2))

    def region(self, s, i, j):
        a, b, sign = self.axes(s)
        at = list(self.at)
        at[a] = lax.rem(at[a] - sign * i + SIDE, SIDE)
        at[b] = lax.rem(at[b] - sign * j + SIDE, SIDE)
        chip = at[0] * SIDE + at[1]
        rows = self.buf.shape[0] // STREAMS
        wide = self.buf.shape[1] // CHIPS
        return self.buf.at[pl.ds(s * rows, rows), pl.ds(pl.multiple_of(chip * wide, wide), wide)]

    def device(self, s, second):
        sign = self.axes(s)[2]
        axis = self.axes(s)[1 if second else 0]
        at = list(self.at)
        at[axis] = lax.rem(at[axis] + sign + SIDE, SIDE)
        return (self.z, (at[0] * SIDE + at[1]) * 2 + self.core)

    def copy(self, s, i, j, second):
        here = self.region(s, i, j)
        k = i * SIDE + j
        return (
            here, here, self.send_sem.at[s, k, second],
            self.recv_sem.at[s, k + (1 if second else SIDE)], self.device(s, second),
        )

    def wave(self, k):
        for i in range(min(k, SIDE - 1), -1, -1):
            j = k - i
            if j >= SIDE:
                continue
            for s in range(STREAMS):
                if k > 0:
                    second = 1 if j else 0
                    came = self.copy(s, i - (1 - second), j - second, second)
                    here = self.region(s, i, j)
                    self.links.copy(here, here, came[2], came[3], came[4]).wait_recv()
                if j == 0 and i < SIDE - 1:
                    self.links.send(*self.copy(s, i, j, 0))
                if j < SIDE - 1:
                    self.links.send(*self.copy(s, i, j, 1))


def lanes(i, width):
    return pl.ds(pl.multiple_of(i * width, width), width)


class Ring:
    def __init__(self, links, count, z, ch):
        self.links, self.count, self.z, self.ch = links, count, z, ch
        self.far = count // 2

    def at(self, way, k):
        return lax.rem(self.z + (1 - 2 * way) * k + 2 * self.count, self.count)

    def next(self, way):
        return (self.at(way, 1), self.ch)

    def hops(self, way, lot):
        return self.far if lot % 2 == way else self.count - 1 - self.far

    def came(self, here, sems, way, lot, step):
        self.links.copy(
            here, here, sems[0].at[way, lot, step], sems[1].at[way, lot, step], self.next(way)
        ).wait_recv()

    def go(self, src, dst, sems, way, lot, step):
        self.links.send(
            src, dst, sems[0].at[way, lot, step], sems[1].at[way, lot, step], self.next(way)
        )

    def spread(self, region, lots, sems):
        for step in range(self.far + 1):
            for lot in range(lots):
                for way in range(2):
                    n = self.hops(way, lot)
                    if step > n:
                        continue
                    here = region(self.at(way, -step), lot)
                    if step > 0:
                        self.came(here, sems, way, lot, step - 1)
                    if step < n:
                        self.go(here, here, sems, way, lot, step)
            yield

    def reduce(self, term, buf, lots, sems, keep):
        for step in range(self.far):
            for lot in range(lots):
                for way in range(2):
                    n = self.hops(way, lot)
                    if step >= n:
                        continue
                    here = buf.at[way, lot, step]
                    value = term(self.at(way, n - step), lot)
                    if step > 0:
                        self.came(here, sems, way, lot, step - 1)
                        value = value + here[...].astype(f32)
                    here[...] = value.astype(bf16)
                    self.go(here, buf.at[way, lot, step + 1], sems, way, lot, step)
            yield
        for lot in range(lots):
            value = term(self.z, lot)
            for way in range(2):
                n = self.hops(way, lot)
                here = buf.at[way, lot, n]
                self.came(here, sems, way, lot, n - 1)
                value = value + here[...].astype(f32)
            keep(lot, value)


def kernel(
    count, lengths, q_in, key_in, val_in, w, d_out, rate_in, res_in, skip_in,
    out, dq, dk, dv, small, dw,
    q, key, val, rate_ref, res_ref, skip, dq_own, dk_own, dv_own,
    G, H, W2, WC, xs, gs, ys, hs, field, dp, dp_send, prod, out_send, out_all,
    states, state_got, small_all, small_sum, dw_own, dw_send, dw_got, ring_buf, dw_all,
    g_send, g_recv, h_send, h_recv, loc, one_s, one_r, a2a_s, a2a_r, wz_s, wz_r,
    st_s, st_r, sm_s, sm_r, rs_s, rs_r, ag_s, ag_r,
):
    z, ch = lax.axis_index("pos"), lax.axis_index("ch")
    core, chip = lax.rem(ch, 2), lax.div(ch, 2)
    x, y = lax.div(chip, SIDE), lax.rem(chip, SIDE)
    mate = (z, chip * 2 + 1 - core)
    other = 1 - core
    t, c = q.shape
    half = t // 2
    wide = 2 * c
    n_out = w.shape[1]

    def along(k):
        return (lax.rem(z + k + count, count), ch)

    def chip_at(k):
        return lax.rem(chip + k, CHIPS)

    barrier = pltpu.get_barrier_semaphore()
    peers = [mate] + [along(k) for k in range(1, count)]
    peers += [(z, chip_at(k) * 2 + core) for k in range(1, CHIPS)]
    for device in peers:
        pl.semaphore_signal(barrier, inc=1, device_id=device, device_id_type=MESH)

    mine, its = lanes(core, half), lanes(other, half)
    own_cols = pl.ds(pl.multiple_of(chip * wide + core * c, c), c)
    mate_cols = pl.ds(pl.multiple_of(chip * wide + other * c, c), c)
    slab = c // count
    own_rows = pl.ds(pl.multiple_of(z * slab, slab), slab)
    slab_rows = pl.ds(pl.multiple_of(core * c + z * slab, slab), slab)
    local = [
        pltpu.make_async_copy(src, dst, loc.at[n])
        for n, (src, dst) in enumerate(
            [
                (d_out.at[mine], G.at[:, own_cols]),
                (key_in, key),
                (val_in, val),
                (rate_in, rate_ref),
                (res_in, res_ref),
                (skip_in, skip),
                (q_in, q),
                (w.at[own_rows, lanes(chip, wide)], WC.at[chip, slab_rows]),
                (w, W2.at[lanes(core, c)]),
            ]
        )
    ]
    for copy in local:
        copy.start()
    pl.semaphore_wait(barrier, len(peers))

    links = Links()
    links.send(d_out.at[its], G.at[:, own_cols], one_s.at[0], one_r.at[0], mate)
    for k in range(1, CHIPS):
        links.send(
            w.at[own_rows, lanes(chip_at(k), wide)], WC.at[chip, slab_rows],
            a2a_s.at[k], a2a_r.at[k], (z, chip_at(k) * 2 + core),
        )

    def got_one(ref, i):
        links.copy(ref, ref, one_s.at[i], one_r.at[i], mate).wait_recv()

    for n in range(1, 6):
        local[n].wait()
    rate, residue = rate_ref[...], res_ref[...]
    xx = key[...].astype(f32) * val[...].astype(f32)
    interleave(xs, xx)
    local[0].wait()
    got_one(G.at[:, mate_cols], 0)
    first = Gather(links, G, g_send, g_recv, z, x, y, core)
    first.wave(0)
    sub = t // NSUB
    p = scan_states(xs, rate, False)
    states[0] = edge_of(p, False)
    for n in (1, 2, 3):
        links.send(
            states.at[0], state_got.at[0, n - 1], st_s.at[0, n - 1], st_r.at[0, n - 1], along(n)
        )
    links.send(w, W2.at[lanes(core, c)], one_s.at[1], one_r.at[1], mate)
    first.wave(1)

    def document(b):
        end, before = lengths[0], jnp.int32(0)
        for n in range(lengths.shape[0]):
            before = before + jnp.where(end <= b, 1, 0)
            if n + 1 < lengths.shape[0]:
                end = end + lengths[n + 1]
        return before

    def carried(way):
        total = None
        for n in (1, 2, 3):
            here = state_got.at[way, n - 1]
            links.copy(here, here, st_s.at[way, n - 1], st_r.at[way, n - 1], mate).wait_recv()
            b = z + n if way else z - n
            same = (b >= 0) & (b < count) & (document(b) == document(z))
            decay = jnp.exp(-rate * float(t * (n - 1))) * jnp.where(same, 1.0, 0.0).astype(f32)
            term = decay * here[...]
            total = term if total is None else total + term
        return total

    start = entering_of(p, rate, sub, carried(0), False)
    forward_pass(xs, ys, hs, rate, residue, start)
    first.wave(2)
    cc = deinterleave(ys) + skip[...] * xx
    field[...] = cc
    local[6].wait()
    prod[...] = (q[...].astype(f32) * cc).astype(bf16)
    links.send(prod.at[its], H.at[:, own_cols], one_s.at[2], one_r.at[2], mate)
    H[:, own_cols] = prod[mine, :]
    first.wave(3)
    local[7].wait()
    for k in range(1, CHIPS):
        here = WC.at[chip_at(CHIPS - k), slab_rows]
        links.copy(here, here, a2a_s.at[k], a2a_r.at[k], mate).wait_recv()
    ring = Ring(links, count, z, ch)
    lot_chips = CHIPS // 2

    def columns(s, lot):
        rows = pl.ds(pl.multiple_of(core * c + s * slab, slab), slab)
        return WC.at[lot * lot_chips : (lot + 1) * lot_chips, rows]

    w_round = ring.spread(columns, 2, (wz_s, wz_r))
    next(w_round)
    got_one(H.at[:, mate_cols], 2)
    second = Gather(links, H, h_send, h_recv, z, x, y, core)
    first.wave(4)
    second.wave(0)
    next(w_round)
    first.wave(5)
    second.wave(1)
    next(w_round)
    first.wave(6)
    second.wave(2)
    next(w_round)

    mate_t = H[:, mate_cols].T
    own_t = H[:, own_cols].T
    both = jnp.concatenate([mate_t, own_t], axis=0)
    block = n_out // 8
    for j in range(8):
        cols = pl.ds(j * block, block)
        r = jnp.dot(both, G[:, cols], preferred_element_type=f32)
        dw_send[:, cols] = r[:c].astype(bf16)
        dw_own[:, cols] = r[c:]
    links.send(dw_send, dw_got, one_s.at[4], one_r.at[4], mate)
    next(w_round)
    links.send(WC.at[:, lanes(core, c)], WC.at[:, lanes(core, c)], one_s.at[5], one_r.at[5], mate)

    local[8].wait()
    got_one(W2.at[lanes(other, c)], 1)
    deep = n_out // 4
    acc = None
    for j in range(4):
        cols = pl.ds(j * deep, deep)
        term = lax.dot_general(
            G[:, cols], W2[:, cols], (((1,), (1,)), ((), ())), preferred_element_type=f32
        )
        acc = term if acc is None else acc + term
    is_first = core == 0
    dp[mine, :] = jnp.where(is_first, acc[:, :c], acc[:, c:])
    dp_send[...] = jnp.where(is_first, acc[:, c:], acc[:, :c])
    links.send(dp_send, dp.at[mine], one_s.at[3], one_r.at[3], mate)
    got_one(dw_got, 4)

    lot_rows = c // LOTS
    span = n_out // count

    def term(s, lot):
        rows, cols = pl.ds(lot * lot_rows, lot_rows), lanes(s, span)
        return dw_own[rows, cols] + dw_got[rows, cols].astype(f32)

    def keep(lot, value):
        dw_all[pl.ds(lot * lot_rows, lot_rows), lanes(z, span)] = value.astype(bf16)

    def block_of(s, lot):
        return dw_all.at[pl.ds(lot * lot_rows, lot_rows), lanes(s, span)]

    def sums():
        yield from ring.reduce(term, ring_buf, LOTS, (rs_s, rs_r), keep)
        yield from ring.spread(block_of, LOTS, (ag_s, ag_r))

    reduce = sums()
    next(reduce)
    second.wave(3)
    got_one(dp.at[its], 3)
    g = dp[...] * q[...].astype(f32)
    interleave(gs, g)
    p = scan_states(gs, rate, True)
    states[1] = edge_of(p, True)
    for n in (1, 2, 3):
        links.send(
            states.at[1], state_got.at[1, n - 1], st_s.at[1, n - 1], st_r.at[1, n - 1], along(-n)
        )
    next(reduce)
    second.wave(4)
    start = entering_of(p, rate, sub, carried(1), True)
    result = []
    back = backward_pieces(xs, gs, ys, hs, rate, residue, start, 2, result)
    next(back)
    next(reduce)
    second.wave(5)
    next(back)
    next(reduce)
    second.wave(6)
    next(back)
    next(reduce)
    next(back)
    next(back, None)

    dskip = jnp.sum(xx * g, axis=0, keepdims=True)
    for n in range(2):
        small_all[z, n * GROUP : (n + 1) * GROUP] = result[n]
        small_all[z, MODES + n * GROUP : MODES + (n + 1) * GROUP] = result[2 + n]
    small_all[z, 2 * MODES :] = jnp.broadcast_to(dskip, (GROUP, c))
    for n in range(1, count):
        links.send(small_all.at[z], small_all.at[z], sm_s.at[n], sm_r.at[n], along(n))
    next(reduce)
    dq_own[...] = (dp[...] * field[...]).astype(bf16)
    dm = deinterleave(ys) + skip[...] * g
    dk_own[...] = (dm * val[...].astype(f32)).astype(bf16)
    dv_own[...] = (dm * key[...].astype(f32)).astype(bf16)
    done = [
        pltpu.make_async_copy(src, dst, loc.at[n])
        for n, (src, dst) in enumerate(
            [(dq_own, dq), (dk_own, dk), (dv_own, dv), (small_sum, small), (out_all, out), (dw_all, dw)]
        )
    ]
    for n in range(3):
        done[n].start()
    next(reduce)

    got_one(WC.at[:, lanes(other, c)], 5)
    acc = None
    for j in range(4):
        per = CHIPS // 4
        part = jnp.dot(
            H[:, pl.ds(j * per * wide, per * wide)],
            WC[j * per : (j + 1) * per].reshape(per * wide, wide),
            preferred_element_type=f32,
        )
        acc = part if acc is None else acc + part
    out_all[mine, :] = jnp.where(is_first, acc[:, :c], acc[:, c:]).astype(bf16)
    out_send[...] = jnp.where(is_first, acc[:, c:], acc[:, :c]).astype(bf16)
    links.send(out_send, out_all.at[mine], one_s.at[6], one_r.at[6], mate)
    for _ in reduce:
        pass
    done[5].start()
    for n in range(1, count):
        here = small_all.at[ring.at(0, -n)]
        links.copy(here, here, sm_s.at[n], sm_r.at[n], mate).wait_recv()
    total = small_all[0]
    for n in range(1, count):
        total = total + small_all[n]
    small_sum[...] = total
    done[3].start()
    got_one(out_all.at[its], 6)
    done[4].start()
    links.drain()
    for copy in done:
        copy.wait()


def finish(out_in, dq_in, dk_in, dv_in, small, dw_in, out, dq, dk, dv, dres, drate, dskip, dw):
    out[...] = out_in[...]
    dq[...] = dq_in[...]
    dk[...] = dk_in[...]
    dv[...] = dv_in[...]
    dres[...] = small[:MODES]
    drate[...] = small[MODES : 2 * MODES]
    dskip[...] = small[2 * MODES : 2 * MODES + 1]
    dw[...] = dw_in[...].astype(f32)


def shards(queries, keys, values, residue, rate, skip, w_out, lengths, d_out):
    t, c = queries.shape
    n_out = w_out.shape[1]
    count = lax.axis_size("pos")
    thin = jax.ShapeDtypeStruct((t, c), bf16)
    rows = 2 * MODES + GROUP
    vmem, dma = pltpu.VMEM, pltpu.SemaphoreType.DMA
    wide, half, far = 2 * c, t // 2, count // 2
    tall, short = vmem((t, c), f32), vmem((t, c), bf16)
    few = vmem((MODES, c), f32)
    scratch = [
        short, short, short, few, few, vmem((1, c), f32), short, short, short,
        vmem((half, n_out), bf16), vmem((half, n_out), bf16), vmem((wide, n_out), bf16),
        vmem((CHIPS, wide, wide), bf16), tall, tall, tall,
        vmem((t // NSUB, MODES, NSUB, c), f32), tall, tall, vmem((half, c), f32),
        short, vmem((half, c), bf16), short,
        vmem((2, MODES, c), f32), vmem((2, 3, MODES, c), f32), vmem((count, rows, c), f32),
        vmem((rows, c), f32),
        vmem((c, n_out), f32), vmem((c, n_out), bf16), vmem((c, n_out), bf16),
        vmem((2, LOTS, far + 1, c // LOTS, n_out // count), bf16), vmem((c, n_out), bf16),
        dma((STREAMS, CHIPS, 2)), dma((STREAMS, CHIPS)), dma((STREAMS, CHIPS, 2)),
        dma((STREAMS, CHIPS)), dma((9,)), dma((7,)), dma((7,)), dma((CHIPS,)), dma((CHIPS,)),
        dma((2, 2, far)), dma((2, 2, far)), dma((2, 3)), dma((2, 3)), dma((count,)), dma((count,)),
        dma((2, LOTS, far)), dma((2, LOTS, far)), dma((2, LOTS, far)), dma((2, LOTS, far)),
    ]
    whole = pl.BlockSpec(memory_space=pltpu.VMEM)
    apart = pl.BlockSpec(memory_space=pl.ANY)
    out, dq, dk, dv, small, dw = pl.pallas_call(
        functools.partial(kernel, count),
        out_shape=(
            thin, thin, thin, thin, jax.ShapeDtypeStruct((rows, c), f32),
            jax.ShapeDtypeStruct((c, n_out), bf16),
        ),
        in_specs=[pl.BlockSpec(memory_space=pltpu.SMEM)] + [apart] * 8,
        out_specs=(apart,) * 6,
        scratch_shapes=scratch,
        compiler_params=pltpu.CompilerParams(
            collective_id=0, has_side_effects=True, vmem_limit_bytes=60 * MIB
        ),
    )(lengths, queries, keys, values, w_out, d_out, rate.T, residue.T, skip[None, :])
    state = jax.ShapeDtypeStruct((MODES, c), f32)
    out, dq, dk, dv, dres, drate, dskip, dw = pl.pallas_call(
        finish,
        out_shape=(
            thin, thin, thin, thin, state, state, jax.ShapeDtypeStruct((1, c), f32),
            jax.ShapeDtypeStruct((c, n_out), f32),
        ),
        in_specs=[whole] * 6,
        out_specs=(whole,) * 8,
        compiler_params=pltpu.CompilerParams(vmem_limit_bytes=60 * MIB),
    )(out, dq, dk, dv, small, dw)
    return out, dq, dk, dv, dres.T, drate.T, dskip[0], dw


def solution(mesh):
    both, chan = P("pos", "ch"), P("ch", None)
    return jax.shard_map(
        shards,
        mesh=mesh,
        in_specs=(both, both, both, chan, chan, P("ch"), chan, P(), both),
        out_specs=(both, both, both, both, chan, chan, P("ch"), chan),
        check_vma=False,
    )
```

```python
import functools

import jax
import jax.numpy as jnp
from jax import lax
from jax.experimental import pallas as pl
from jax.experimental.pallas import tpu as pltpu
from jax.sharding import PartitionSpec as P

f32 = jnp.float32
bf16 = jnp.bfloat16
MODES = 16
GROUP = 8
NSUB = 8
UNROLL = 4
SIDE = 4
CHIPS = SIDE * SIDE
MESH = pl.DeviceIdType.MESH
MIB = 1024 * 1024


def rows_of(s):
    return pl.ds(pl.multiple_of(s * NSUB, NSUB), NSUB)


def interleave(dst, val):
    sub = val.shape[0] // NSUB
    for n in range(NSUB):
        dst[pl.ds(n, sub, stride=NSUB), :] = val[n * sub : (n + 1) * sub]


def deinterleave(src):
    sub = src.shape[0] // NSUB
    return jnp.concatenate([src[pl.ds(n, sub, stride=NSUB), :] for n in range(NSUB)], axis=0)


def spread(a):
    return jnp.broadcast_to(a[:, None, :], (a.shape[0], NSUB, a.shape[1]))


def place_of(shape):
    return lax.broadcasted_iota(jnp.int32, shape, 1)


def scan_states(src, rate, reverse):
    sub = src.shape[0] // NSUB
    lam = spread(jnp.exp(-rate))

    def step(i, h):
        s = sub - 1 - i if reverse else i
        return lam * h + src[rows_of(s), :][None]

    p = lax.fori_loop(0, sub, step, jnp.zeros_like(lam), unroll=UNROLL)
    place = place_of(p.shape)
    for k in (1, 2, 4):
        moved = pltpu.roll(p, NSUB - k if reverse else k, 1)
        ok = place < NSUB - k if reverse else place >= k
        p = p + spread(jnp.exp(-rate * (sub * k))) * jnp.where(ok, moved, 0.0)
    return p


def edge_of(p, reverse):
    return jnp.sum(jnp.where(place_of(p.shape) == (0 if reverse else NSUB - 1), p, 0.0), axis=1)


def entering_of(p, rate, sub, carry, reverse):
    place = place_of(p.shape)
    moved = pltpu.roll(p, NSUB - 1 if reverse else 1, 1)
    ok = place < NSUB - 1 if reverse else place >= 1
    steps = (NSUB - 1 - place if reverse else place).astype(f32) * float(sub)
    return jnp.where(ok, moved, 0.0) + jnp.exp(-spread(rate) * steps) * spread(carry)


def forward_pass(xs, ys, hs, rate, residue, start):
    sub = xs.shape[0] // NSUB
    for lo in range(0, MODES, GROUP):
        part = slice(lo, lo + GROUP)
        lam, res = spread(jnp.exp(-rate[part])), spread(residue[part])

        def step(s, h):
            hs[s, part] = h
            h = lam * h + xs[rows_of(s), :][None]
            y = jnp.sum(res * h, axis=0)
            ys[rows_of(s), :] = y if lo == 0 else ys[rows_of(s), :] + y
            return h

        lax.fori_loop(0, sub, step, start[part], unroll=UNROLL)


def backward_pieces(xs, gs, ms, hs, rate, residue, start, pieces, result):
    sub = xs.shape[0] // NSUB
    span = sub // pieces
    d_res, d_rate = [], []
    for lo in range(0, MODES, GROUP):
        part = slice(lo, lo + GROUP)
        lam, res = spread(jnp.exp(-rate[part])), spread(residue[part])

        def step(i, carry):
            a, dr, dt = carry
            s = sub - 1 - i
            a = lam * a + gs[rows_of(s), :][None]
            m = jnp.sum(res * a, axis=0)
            ms[rows_of(s), :] = m if lo == 0 else ms[rows_of(s), :] + m
            return a, dr + a * xs[rows_of(s), :][None], dt + a * hs[s, part]

        zero = jnp.zeros_like(lam)
        carry = (start[part], zero, zero)
        for piece in range(pieces):
            carry = lax.fori_loop(piece * span, (piece + 1) * span, step, carry, unroll=UNROLL)
            yield
        d_res.append(jnp.sum(carry[1], axis=1))
        d_rate.append(-residue[part] * jnp.exp(-rate[part]) * jnp.sum(carry[2], axis=1))
    result.extend(d_res + d_rate)


class Links:
    def __init__(self):
        self.sent = []

    def copy(self, src, dst, send, recv, device):
        return pltpu.make_async_remote_copy(
            src_ref=src, dst_ref=dst, send_sem=send, recv_sem=recv,
            device_id=device, device_id_type=MESH,
        )

    def send(self, *args):
        c = self.copy(*args)
        c.start()
        self.sent.append(c)

    def drain(self):
        for c in self.sent:
            c.wait_send()
        self.sent = []


NEAR = (-1, 0, 1, 2)
FULL, LOW, HIGH = range(3)
KEYS = [(1, 0, FULL), (-1, 0, FULL), (2, 0, LOW), (2, 0, HIGH)]
for i in (0, 1, -1, 2):
    KEYS += [(i, 1, FULL), (i, -1, FULL), (i, 2, LOW), (i, 2, HIGH)]
OFFSETS = sorted([(i, j) for i in NEAR for j in NEAR], key=lambda o: abs(o[0]) + abs(o[1]))
SCHEDULE = (
    "tw", "g0", "f2", "t0w", "g1", "p0", "f3", "t01w", "s0", "f4", "g2", "p1", "t01w", "bs",
    "t012w", "s1", "be", "t012w", "b", "b", "t012w", "b", "b", "t012", "s2", "b", "bz", "t012",
    "t012", "t012", "s3", "t012", "o0", "t012", "s4", "t012", "o1",
)
GROUPS = [((0, 3), (3, 5)), ((5, 8), (8, 11)), ((11, 13), (13, 16))]


class Gather:
    def __init__(self, links, buf, send, recv, z, x, y, core):
        self.links, self.buf, self.send_sem, self.recv_sem = links, buf, send, recv
        self.z, self.at, self.core = z, (x, y), core

    def region(self, kind, i, j, part):
        at = list(self.at)
        at[kind] = lax.rem(at[kind] + i + SIDE, SIDE)
        at[1 - kind] = lax.rem(at[1 - kind] + j + SIDE, SIDE)
        rows = self.buf.shape[0] // 2
        start = kind * rows + (rows // 2 if part == HIGH else 0)
        wide = self.buf.shape[1] // CHIPS
        return self.buf.at[
            pl.ds(start, rows if part == FULL else rows // 2), lanes(at[0] * SIDE + at[1], wide)
        ]

    def device(self, axis, sign):
        at = list(self.at)
        at[axis] = lax.rem(at[axis] + sign + SIDE, SIDE)
        return (self.z, (at[0] * SIDE + at[1]) * 2 + self.core)

    def send(self, kind, i, j, part):
        n = KEYS.index((i, j, part))
        step = {LOW: 1, HIGH: -1}.get(part, 0)
        away = j if j else i
        sign = -step if step else -away
        here = self.region(kind, i, step, part) if j else self.region(kind, step, 0, part)
        self.links.send(
            here, here, self.send_sem.at[kind, n], self.recv_sem.at[kind, n],
            self.device(1 - kind if j else kind, sign),
        )

    def got(self, kind, i, j, part):
        n = KEYS.index((i, j, part))
        here = self.region(kind, i, j, part)
        self.links.copy(
            here, here, self.send_sem.at[kind, n], self.recv_sem.at[kind, n], self.device(kind, 1)
        ).wait_recv()

    def wave(self, k):
        for i in (1, -1, 2, 0):
            for j in (0, 1, -1, 2):
                if abs(i) + abs(j) != k:
                    continue
                for kind in range(2):
                    for part in (LOW, HIGH) if 2 in (i, j) and (j == 2 or j == 0) else (FULL,):
                        if k > 0:
                            self.got(kind, i, j, part)
                    if k == 0:
                        self.send(kind, 1, 0, FULL)
                        self.send(kind, -1, 0, FULL)
                    elif j == 0 and abs(i) == 1:
                        self.send(kind, 2, 0, LOW if i == 1 else HIGH)
                    if j == 0:
                        self.send(kind, i, 1, FULL)
                        self.send(kind, i, -1, FULL)
                    elif abs(j) == 1:
                        self.send(kind, i, 2, LOW if j == 1 else HIGH)


def lanes(i, width):
    return pl.ds(pl.multiple_of(i * width, width), width)


class Ring:
    def __init__(self, links, count, z, ch):
        self.links, self.count, self.z, self.ch = links, count, z, ch
        self.far = count // 2

    def at(self, way, k):
        return lax.rem(self.z + (1 - 2 * way) * k + 2 * self.count, self.count)

    def next(self, way):
        return (self.at(way, 1), self.ch)

    def hops(self, way, lot):
        return self.far if lot % 2 == way else self.count - 1 - self.far

    def came(self, here, sems, way, lot, step):
        self.links.copy(
            here, here, sems[0].at[way, lot, step], sems[1].at[way, lot, step], self.next(way)
        ).wait_recv()

    def go(self, src, dst, sems, way, lot, step):
        self.links.send(
            src, dst, sems[0].at[way, lot, step], sems[1].at[way, lot, step], self.next(way)
        )

    def spread(self, region, lots, sems):
        for step in range(self.far + 1):
            for lot in range(lots):
                for way in range(2):
                    n = self.hops(way, lot)
                    if step > n:
                        continue
                    here = region(self.at(way, -step), lot)
                    if step > 0:
                        self.came(here, sems, way, lot, step - 1)
                    if step < n:
                        self.go(here, here, sems, way, lot, step)
            yield

    def reduce(self, term, slot, lots, sems, keep):
        for step in range(self.far):
            for lot in range(lots):
                for way in range(2):
                    n = self.hops(way, lot)
                    if step >= n:
                        continue
                    here = slot(way, lot, step)
                    value = term(self.at(way, n - step), lot)
                    if step > 0:
                        self.came(here, sems, way, lot, step - 1)
                        value = value + here[...].astype(f32)
                    here[...] = value.astype(bf16)
                    self.go(here, slot(way, lot, step + 1), sems, way, lot, step)
            yield
        for lot in range(lots):
            value = term(self.z, lot)
            for way in range(2):
                n = self.hops(way, lot)
                here = slot(way, lot, n)
                self.came(here, sems, way, lot, n - 1)
                value = value + here[...].astype(f32)
            keep(lot, value)


def kernel(
    count, lengths, q_in, key_in, val_in, w, d_out, rate_in, res_in, skip_in,
    out, dq, dk, dv, small, dw,
    q, key, val, rate_ref, res_ref, skip, dq_own, dk_own, dv_own,
    G, H, W2, WC, xs, gs, ys, hs, field, dp, dp_send, prod, out_send, out_all,
    states, state_got, small_all, small_sum, dw_own, dw_send, dw_got, ring_buf, dw_all,
    g_send, g_recv, h_send, h_recv, loc, one_s, one_r, a2a_s, a2a_r, wz_s, wz_r,
    st_s, st_r, sm_s, sm_r, rs_s, rs_r, ag_s, ag_r, acc_ref, dw_sem,
):
    z, ch = lax.axis_index("pos"), lax.axis_index("ch")
    core, chip = lax.rem(ch, 2), lax.div(ch, 2)
    x, y = lax.div(chip, SIDE), lax.rem(chip, SIDE)
    mate = (z, chip * 2 + 1 - core)
    other = 1 - core
    t, c = q.shape
    half = t // 2
    wide = 2 * c
    n_out = w.shape[1]

    def along(k):
        return (lax.rem(z + k + count, count), ch)

    def chip_at(k):
        return lax.rem(chip + k, CHIPS)

    barrier = pltpu.get_barrier_semaphore()
    peers = [mate] + [along(k) for k in range(1, count)]
    peers += [(z, chip_at(k) * 2 + core) for k in range(1, CHIPS)]
    for device in peers:
        pl.semaphore_signal(barrier, inc=1, device_id=device, device_id_type=MESH)

    mine, its = lanes(core, half), lanes(other, half)
    own_cols = pl.ds(pl.multiple_of(chip * wide + core * c, c), c)
    mate_cols = pl.ds(pl.multiple_of(chip * wide + other * c, c), c)
    slab = c // count
    own_rows = pl.ds(pl.multiple_of(z * slab, slab), slab)
    slab_rows = pl.ds(pl.multiple_of(core * c + z * slab, slab), slab)
    local = [
        pltpu.make_async_copy(src, dst, loc.at[n])
        for n, (src, dst) in enumerate(
            [
                (d_out.at[mine], G.at[:, own_cols]),
                (key_in, key),
                (val_in, val),
                (rate_in, rate_ref),
                (res_in, res_ref),
                (skip_in, skip),
                (q_in, q),
                (w.at[own_rows, lanes(chip, wide)], WC.at[chip, slab_rows]),
                (w, W2.at[lanes(core, c)]),
            ]
        )
    ]
    for copy in local:
        copy.start()
    pl.semaphore_wait(barrier, len(peers))

    links = Links()
    links.send(d_out.at[its], G.at[:, own_cols], one_s.at[0], one_r.at[0], mate)
    for k in range(1, CHIPS):
        links.send(
            w.at[own_rows, lanes(chip_at(k), wide)], WC.at[chip, slab_rows],
            a2a_s.at[k], a2a_r.at[k], (z, chip_at(k) * 2 + core),
        )

    def got_one(ref, i):
        links.copy(ref, ref, one_s.at[i], one_r.at[i], mate).wait_recv()

    for n in range(1, 6):
        local[n].wait()
    rate, residue = rate_ref[...], res_ref[...]
    xx = key[...].astype(f32) * val[...].astype(f32)
    interleave(xs, xx)
    local[0].wait()
    got_one(G.at[:, mate_cols], 0)
    first = Gather(links, G, g_send, g_recv, z, x, y, core)
    first.wave(0)
    sub = t // NSUB
    p = scan_states(xs, rate, False)
    states[0] = edge_of(p, False)
    for n in (1, 2, 3):
        links.send(
            states.at[0], state_got.at[0, n - 1], st_s.at[0, n - 1], st_r.at[0, n - 1], along(n)
        )
    links.send(w, W2.at[lanes(core, c)], one_s.at[1], one_r.at[1], mate)

    def document(b):
        end, before = lengths[0], jnp.int32(0)
        for n in range(lengths.shape[0]):
            before = before + jnp.where(end <= b, 1, 0)
            if n + 1 < lengths.shape[0]:
                end = end + lengths[n + 1]
        return before

    def carried(way):
        total = None
        for n in (1, 2, 3):
            here = state_got.at[way, n - 1]
            links.copy(here, here, st_s.at[way, n - 1], st_r.at[way, n - 1], mate).wait_recv()
            b = z + n if way else z - n
            same = (b >= 0) & (b < count) & (document(b) == document(z))
            decay = jnp.exp(-rate * float(t * (n - 1))) * jnp.where(same, 1.0, 0.0).astype(f32)
            term = decay * here[...]
            total = term if total is None else total + term
        return total

    start = entering_of(p, rate, sub, carried(0), False)
    forward_pass(xs, ys, hs, rate, residue, start)
    first.wave(1)
    cc = deinterleave(ys) + skip[...] * xx
    field[...] = cc
    local[6].wait()
    prod[...] = (q[...].astype(f32) * cc).astype(bf16)
    links.send(prod.at[its], H.at[:, own_cols], one_s.at[2], one_r.at[2], mate)
    H[:, own_cols] = prod[mine, :]
    ring = Ring(links, count, z, ch)
    lot_chips = CHIPS // 2

    def columns(s, lot):
        rows = pl.ds(pl.multiple_of(core * c + s * slab, slab), slab)
        return WC.at[lot * lot_chips : (lot + 1) * lot_chips, rows]

    got_one(H.at[:, mate_cols], 2)
    second = Gather(links, H, h_send, h_recv, z, x, y, core)

    def chip_of(p):
        i, j = OFFSETS[p]
        return lax.rem(x + i + SIDE, SIDE) * SIDE + lax.rem(y + j + SIDE, SIDE)

    both = jnp.concatenate([H[:, mate_cols].T, H[:, own_cols].T], axis=0)

    def packed(first_one, last):
        return pl.ds(first_one * wide, (last - first_one) * wide)

    def weight_part(group):
        lots = GROUPS[group]
        for p in range(lots[0][0], lots[-1][1]):
            r = jnp.dot(both, G[:, lanes(chip_of(p), wide)], preferred_element_type=f32)
            dw_send[:, packed(p, p + 1)] = r[:c].astype(bf16)
            dw_own[:, packed(p, p + 1)] = r[c:]
        cols = packed(lots[0][0], lots[-1][1])
        links.send(
            dw_send.at[:, cols], dw_got.at[:, cols], one_s.at[7 + group], one_r.at[7 + group], mate
        )

    def sums(group):
        lots = GROUPS[group]
        cols = packed(lots[0][0], lots[-1][1])
        got_one(dw_got.at[:, cols], 7 + group)

        def term(s, lot):
            rows, part = lanes(s, slab), packed(*lots[lot])
            return dw_own[rows, part] + dw_got[rows, part].astype(f32)

        def slot(way, lot, step):
            return ring_buf.at[
                group, way, lot, step, :, pl.ds(0, (lots[lot][1] - lots[lot][0]) * wide)
            ]

        def keep(lot, value):
            dw_all[lanes(z, slab), packed(*lots[lot])] = value.astype(bf16)

        def block_of(s, lot):
            return dw_all.at[lanes(s, slab), packed(*lots[lot])]

        yield from ring.reduce(term, slot, 2, (rs_s.at[group], rs_r.at[group]), keep)
        yield from ring.spread(block_of, 2, (ag_s.at[group], ag_r.at[group]))
        for p in range(lots[0][0], lots[-1][1]):
            copy = pltpu.make_async_copy(
                dw_all.at[:, packed(p, p + 1)], dw.at[:, lanes(chip_of(p), wide)], dw_sem.at[p]
            )
            copy.start()
            done.append(copy)

    done = []

    def weight_columns():
        local[7].wait()
        for k in range(1, CHIPS):
            here = WC.at[chip_at(CHIPS - k), slab_rows]
            links.copy(here, here, a2a_s.at[k], a2a_r.at[k], mate).wait_recv()
        yield from ring.spread(columns, 2, (wz_s, wz_r))
        links.send(
            WC.at[:, lanes(core, c)], WC.at[:, lanes(core, c)], one_s.at[5], one_r.at[5], mate
        )

    rounds = {"w": weight_columns(), "0": sums(0), "1": sums(1), "2": sums(2)}

    def product_part(lo, hi, acc):
        for p in range(lo, hi):
            cols = lanes(chip_of(p), wide)
            part = lax.dot_general(
                G[:, cols], W2[:, cols], (((1,), (1,)), ((), ())), preferred_element_type=f32
            )
            acc = part if acc is None else acc + part
        return acc

    def out_part(lo, hi, acc):
        for p in range(lo, hi):
            part = jnp.dot(
                H[:, lanes(chip_of(p), wide)], WC[chip_of(p)], preferred_element_type=f32
            )
            acc = part if acc is None else acc + part
        return acc

    near = GROUPS[1][-1][1]
    is_first = core == 0

    def product_near():
        local[8].wait()
        got_one(W2.at[lanes(other, c)], 1)
        acc_ref[...] = product_part(0, near, None)

    def product_far():
        acc = product_part(near, CHIPS, acc_ref[...])
        dp[mine, :] = jnp.where(is_first, acc[:, :c], acc[:, c:])
        dp_send[...] = jnp.where(is_first, acc[:, c:], acc[:, :c])
        links.send(dp_send, dp.at[mine], one_s.at[3], one_r.at[3], mate)

    kept = {}

    def back_states():
        got_one(dp.at[its], 3)
        g = dp[...] * q[...].astype(f32)
        interleave(gs, g)
        kept["g"] = g
        kept["p"] = scan_states(gs, rate, True)
        states[1] = edge_of(kept["p"], True)
        for n in (1, 2, 3):
            links.send(
                states.at[1], state_got.at[1, n - 1], st_s.at[1, n - 1], st_r.at[1, n - 1], along(-n)
            )

    def back_start():
        start = entering_of(kept["p"], rate, sub, carried(1), True)
        kept["sums"] = []
        kept["back"] = backward_pieces(xs, gs, ys, hs, rate, residue, start, 2, kept["sums"])

    def back_piece():
        next(kept["back"], None)

    def back_end():
        g, result = kept["g"], kept["sums"]
        dskip = jnp.sum(xx * g, axis=0, keepdims=True)
        for n in range(2):
            small_all[z, n * GROUP : (n + 1) * GROUP] = result[n]
            small_all[z, MODES + n * GROUP : MODES + (n + 1) * GROUP] = result[2 + n]
        small_all[z, 2 * MODES :] = jnp.broadcast_to(dskip, (GROUP, c))
        for n in range(1, count):
            links.send(small_all.at[z], small_all.at[z], sm_s.at[n], sm_r.at[n], along(n))
        dq_own[...] = (dp[...] * field[...]).astype(bf16)
        dm = deinterleave(ys) + skip[...] * g
        dk_own[...] = (dm * val[...].astype(f32)).astype(bf16)
        dv_own[...] = (dm * key[...].astype(f32)).astype(bf16)
        for n, (src, dst) in enumerate([(dq_own, dq), (dk_own, dk), (dv_own, dv)]):
            copy = pltpu.make_async_copy(src, dst, loc.at[n])
            copy.start()
            done.append(copy)

    def out_near():
        for _ in rounds["w"]:
            pass
        got_one(WC.at[:, lanes(other, c)], 5)
        acc_ref[...] = out_part(0, near, None)

    def out_far():
        acc = out_part(near, CHIPS, acc_ref[...])
        out_all[mine, :] = jnp.where(is_first, acc[:, :c], acc[:, c:]).astype(bf16)
        out_send[...] = jnp.where(is_first, acc[:, c:], acc[:, :c]).astype(bf16)
        links.send(out_send, out_all.at[mine], one_s.at[6], one_r.at[6], mate)

    tasks = {
        "p0": product_near, "p1": product_far, "bs": back_states, "be": back_start,
        "b": back_piece, "bz": back_end, "o0": out_near, "o1": out_far,
    }
    for name in SCHEDULE:
        if name in tasks:
            tasks[name]()
        elif name[0] == "g":
            weight_part(int(name[1]))
        elif name[0] == "f":
            first.wave(int(name[1]))
        elif name[0] == "s":
            second.wave(int(name[1]))
        else:
            for one in name[1:]:
                next(rounds[one], None)
    for one in rounds.values():
        for _ in one:
            pass
    for n in range(1, count):
        here = small_all.at[ring.at(0, -n)]
        links.copy(here, here, sm_s.at[n], sm_r.at[n], mate).wait_recv()
    total = small_all[0]
    for n in range(1, count):
        total = total + small_all[n]
    small_sum[...] = total
    got_one(out_all.at[its], 6)
    for n, (src, dst) in enumerate([(small_sum, small), (out_all, out)]):
        copy = pltpu.make_async_copy(src, dst, loc.at[3 + n])
        copy.start()
        done.append(copy)
    links.drain()
    for copy in done:
        copy.wait()


def finish(out_in, dq_in, dk_in, dv_in, small, dw_in, out, dq, dk, dv, dres, drate, dskip, dw, thin, taken, given, sems):
    runs = 4
    rows = taken.shape[0] // runs
    parts = [pl.ds(n * rows, rows) for n in range(runs)]
    wide_in = [
        pltpu.make_async_copy(dw_in.at[part], taken.at[part], sems.at[0, n])
        for n, part in enumerate(parts)
    ]
    thin_in = [
        pltpu.make_async_copy(src, thin.at[n], sems.at[1, n])
        for n, src in enumerate((out_in, dq_in, dk_in, dv_in))
    ]
    wide_out = [
        pltpu.make_async_copy(given.at[part], dw.at[part], sems.at[2, n])
        for n, part in enumerate(parts)
    ]
    thin_out = [
        pltpu.make_async_copy(thin.at[n], dst, sems.at[3, n])
        for n, dst in enumerate((out, dq, dk, dv))
    ]
    for copy in wide_in + thin_in:
        copy.start()
    dres[...] = small[:MODES]
    drate[...] = small[MODES : 2 * MODES]
    dskip[...] = small[2 * MODES : 2 * MODES + 1]
    for n, part in enumerate(parts):
        wide_in[n].wait()
        given[part, :] = taken[part, :].astype(f32)
        wide_out[n].start()
        thin_in[n].wait()
        thin_out[n].start()
    for copy in wide_out + thin_out:
        copy.wait()


def shards(queries, keys, values, residue, rate, skip, w_out, lengths, d_out):
    t, c = queries.shape
    n_out = w_out.shape[1]
    count = lax.axis_size("pos")
    thin = jax.ShapeDtypeStruct((t, c), bf16)
    rows = 2 * MODES + GROUP
    vmem, dma = pltpu.VMEM, pltpu.SemaphoreType.DMA
    wide, half, far = 2 * c, t // 2, count // 2
    tall, short = vmem((t, c), f32), vmem((t, c), bf16)
    few = vmem((MODES, c), f32)
    scratch = [
        short, short, short, few, few, vmem((1, c), f32), short, short, short,
        vmem((half, n_out), bf16), vmem((half, n_out), bf16), vmem((wide, n_out), bf16),
        vmem((CHIPS, wide, wide), bf16), tall, tall, tall,
        vmem((t // NSUB, MODES, NSUB, c), f32), tall, tall, vmem((half, c), f32),
        short, vmem((half, c), bf16), short,
        vmem((2, MODES, c), f32), vmem((2, 3, MODES, c), f32), vmem((count, rows, c), f32),
        vmem((rows, c), f32),
        vmem((c, n_out), f32), vmem((c, n_out), bf16), vmem((c, n_out), bf16),
        vmem((3, 2, 2, far + 1, c // count, 3 * wide), bf16), vmem((c, n_out), bf16),
        dma((2, len(KEYS))), dma((2, len(KEYS))), dma((2, len(KEYS))), dma((2, len(KEYS))),
        dma((9,)), dma((10,)), dma((10,)), dma((CHIPS,)), dma((CHIPS,)),
        dma((2, 2, far)), dma((2, 2, far)), dma((2, 3)), dma((2, 3)), dma((count,)), dma((count,)),
        dma((3, 2, 2, far)), dma((3, 2, 2, far)), dma((3, 2, 2, far)), dma((3, 2, 2, far)),
        vmem((half, wide), f32), dma((CHIPS,)),
    ]
    whole = pl.BlockSpec(memory_space=pltpu.VMEM)
    apart = pl.BlockSpec(memory_space=pl.ANY)
    out, dq, dk, dv, small, dw = pl.pallas_call(
        functools.partial(kernel, count),
        out_shape=(
            thin, thin, thin, thin, jax.ShapeDtypeStruct((rows, c), f32),
            jax.ShapeDtypeStruct((c, n_out), bf16),
        ),
        in_specs=[pl.BlockSpec(memory_space=pltpu.SMEM)] + [apart] * 8,
        out_specs=(apart,) * 6,
        scratch_shapes=scratch,
        compiler_params=pltpu.CompilerParams(
            collective_id=0, has_side_effects=True, vmem_limit_bytes=60 * MIB
        ),
    )(lengths, queries, keys, values, w_out, d_out, rate.T, residue.T, skip[None, :])
    state = jax.ShapeDtypeStruct((MODES, c), f32)
    out, dq, dk, dv, dres, drate, dskip, dw = pl.pallas_call(
        finish,
        out_shape=(
            thin, thin, thin, thin, state, state, jax.ShapeDtypeStruct((1, c), f32),
            jax.ShapeDtypeStruct((c, n_out), f32),
        ),
        in_specs=[apart] * 4 + [whole, apart],
        out_specs=(apart,) * 4 + (whole,) * 3 + (apart,),
        scratch_shapes=[
            vmem((4, t, c), bf16), vmem((c, n_out), bf16), vmem((c, n_out), f32), dma((4, 4)),
        ],
        compiler_params=pltpu.CompilerParams(vmem_limit_bytes=60 * MIB),
    )(out, dq, dk, dv, small, dw)
    return out, dq, dk, dv, dres.T, drate.T, dskip[0], dw


def solution(mesh):
    both, chan = P("pos", "ch"), P("ch", None)
    return jax.shard_map(
        shards,
        mesh=mesh,
        in_specs=(both, both, both, chan, chan, P("ch"), chan, P(), both),
        out_specs=(both, both, both, both, chan, chan, P("ch"), chan),
        check_vma=False,
    )
```

```python
import functools

import jax
import jax.numpy as jnp
from jax import lax
from jax.experimental import pallas as pl
from jax.experimental.pallas import tpu as pltpu
from jax.sharding import PartitionSpec as P

f32 = jnp.float32
bf16 = jnp.bfloat16
MODES = 16
GROUP = 8
NSUB = 8
UNROLL = 4
SIDE = 4
CHIPS = SIDE * SIDE
MESH = pl.DeviceIdType.MESH
MIB = 1024 * 1024


def rows_of(s):
    return pl.ds(pl.multiple_of(s * NSUB, NSUB), NSUB)


def interleave(dst, val):
    sub = val.shape[0] // NSUB
    for n in range(NSUB):
        dst[pl.ds(n, sub, stride=NSUB), :] = val[n * sub : (n + 1) * sub]


def deinterleave(src):
    sub = src.shape[0] // NSUB
    return jnp.concatenate([src[pl.ds(n, sub, stride=NSUB), :] for n in range(NSUB)], axis=0)


def spread(a):
    return jnp.broadcast_to(a[:, None, :], (a.shape[0], NSUB, a.shape[1]))


def place_of(shape):
    return lax.broadcasted_iota(jnp.int32, shape, 1)


def scan_states(src, rate, reverse):
    sub = src.shape[0] // NSUB
    lam = spread(jnp.exp(-rate))

    def step(i, h):
        s = sub - 1 - i if reverse else i
        return lam * h + src[rows_of(s), :][None]

    p = lax.fori_loop(0, sub, step, jnp.zeros_like(lam), unroll=UNROLL)
    place = place_of(p.shape)
    for k in (1, 2, 4):
        moved = pltpu.roll(p, NSUB - k if reverse else k, 1)
        ok = place < NSUB - k if reverse else place >= k
        p = p + spread(jnp.exp(-rate * (sub * k))) * jnp.where(ok, moved, 0.0)
    return p


def edge_of(p, reverse):
    return jnp.sum(jnp.where(place_of(p.shape) == (0 if reverse else NSUB - 1), p, 0.0), axis=1)


def entering_of(p, rate, sub, carry, reverse):
    place = place_of(p.shape)
    moved = pltpu.roll(p, NSUB - 1 if reverse else 1, 1)
    ok = place < NSUB - 1 if reverse else place >= 1
    steps = (NSUB - 1 - place if reverse else place).astype(f32) * float(sub)
    return jnp.where(ok, moved, 0.0) + jnp.exp(-spread(rate) * steps) * spread(carry)


def forward_pass(xs, ys, hs, rate, residue, start):
    sub = xs.shape[0] // NSUB
    for lo in range(0, MODES, GROUP):
        part = slice(lo, lo + GROUP)
        lam, res = spread(jnp.exp(-rate[part])), spread(residue[part])

        def step(s, h):
            hs[s, part] = h
            h = lam * h + xs[rows_of(s), :][None]
            y = jnp.sum(res * h, axis=0)
            ys[rows_of(s), :] = y if lo == 0 else ys[rows_of(s), :] + y
            return h

        lax.fori_loop(0, sub, step, start[part], unroll=UNROLL)


def backward_pieces(xs, gs, ms, hs, rate, residue, start, pieces, result):
    sub = xs.shape[0] // NSUB
    span = sub // pieces
    d_res, d_rate = [], []
    for lo in range(0, MODES, GROUP):
        part = slice(lo, lo + GROUP)
        lam, res = spread(jnp.exp(-rate[part])), spread(residue[part])

        def step(i, carry):
            a, dr, dt = carry
            s = sub - 1 - i
            a = lam * a + gs[rows_of(s), :][None]
            m = jnp.sum(res * a, axis=0)
            ms[rows_of(s), :] = m if lo == 0 else ms[rows_of(s), :] + m
            return a, dr + a * xs[rows_of(s), :][None], dt + a * hs[s, part]

        zero = jnp.zeros_like(lam)
        carry = (start[part], zero, zero)
        for piece in range(pieces):
            carry = lax.fori_loop(piece * span, (piece + 1) * span, step, carry, unroll=UNROLL)
            yield
        d_res.append(jnp.sum(carry[1], axis=1))
        d_rate.append(-residue[part] * jnp.exp(-rate[part]) * jnp.sum(carry[2], axis=1))
    result.extend(d_res + d_rate)


class Links:
    def __init__(self):
        self.sent = []

    def copy(self, src, dst, send, recv, device):
        return pltpu.make_async_remote_copy(
            src_ref=src, dst_ref=dst, send_sem=send, recv_sem=recv,
            device_id=device, device_id_type=MESH,
        )

    def send(self, *args):
        c = self.copy(*args)
        c.start()
        self.sent.append(c)

    def drain(self):
        for c in self.sent:
            c.wait_send()
        self.sent = []


NEAR = (-1, 0, 1, 2)
FULL, LOW, HIGH = range(3)
KEYS = [(1, 0, FULL), (-1, 0, FULL), (2, 0, LOW), (2, 0, HIGH)]
for i in (0, 1, -1, 2):
    KEYS += [(i, 1, FULL), (i, -1, FULL), (i, 2, LOW), (i, 2, HIGH)]
OFFSETS = sorted([(i, j) for i in NEAR for j in NEAR], key=lambda o: abs(o[0]) + abs(o[1]))
SCHEDULE = (
    "tw", "g0", "f2", "t0w", "g1", "p0", "f3", "t01w", "s0", "f4", "g2", "p1", "t012w", "bs",
    "t012w", "s1", "be", "t012w", "b", "b", "t012w", "b", "b", "t012", "s2", "b", "bz", "t012",
    "t012", "s3", "t012", "o0", "t012", "s4", "t012", "o1",
)
GROUPS = [((0, 3), (3, 5)), ((5, 8), (8, 11)), ((11, 13), (13, 16))]


class Gather:
    def __init__(self, links, buf, send, recv, z, x, y, core):
        self.links, self.buf, self.send_sem, self.recv_sem = links, buf, send, recv
        self.z, self.at, self.core = z, (x, y), core

    def region(self, kind, i, j, part):
        at = list(self.at)
        at[kind] = lax.rem(at[kind] + i + SIDE, SIDE)
        at[1 - kind] = lax.rem(at[1 - kind] + j + SIDE, SIDE)
        rows = self.buf.shape[0] // 2
        start = kind * rows + (rows // 2 if part == HIGH else 0)
        wide = self.buf.shape[1] // CHIPS
        return self.buf.at[
            pl.ds(start, rows if part == FULL else rows // 2), lanes(at[0] * SIDE + at[1], wide)
        ]

    def device(self, axis, sign):
        at = list(self.at)
        at[axis] = lax.rem(at[axis] + sign + SIDE, SIDE)
        return (self.z, (at[0] * SIDE + at[1]) * 2 + self.core)

    def send(self, kind, i, j, part):
        n = KEYS.index((i, j, part))
        step = {LOW: 1, HIGH: -1}.get(part, 0)
        away = j if j else i
        sign = -step if step else -away
        here = self.region(kind, i, step, part) if j else self.region(kind, step, 0, part)
        self.links.send(
            here, here, self.send_sem.at[kind, n], self.recv_sem.at[kind, n],
            self.device(1 - kind if j else kind, sign),
        )

    def got(self, kind, i, j, part):
        n = KEYS.index((i, j, part))
        here = self.region(kind, i, j, part)
        self.links.copy(
            here, here, self.send_sem.at[kind, n], self.recv_sem.at[kind, n], self.device(kind, 1)
        ).wait_recv()

    def wave(self, k):
        for i in (1, -1, 2, 0):
            for j in (0, 1, -1, 2):
                if abs(i) + abs(j) != k:
                    continue
                for kind in range(2):
                    for part in (LOW, HIGH) if 2 in (i, j) and (j == 2 or j == 0) else (FULL,):
                        if k > 0:
                            self.got(kind, i, j, part)
                    if k == 0:
                        self.send(kind, 1, 0, FULL)
                        self.send(kind, -1, 0, FULL)
                    elif j == 0 and abs(i) == 1:
                        self.send(kind, 2, 0, LOW if i == 1 else HIGH)
                    if j == 0:
                        self.send(kind, i, 1, FULL)
                        self.send(kind, i, -1, FULL)
                    elif abs(j) == 1:
                        self.send(kind, i, 2, LOW if j == 1 else HIGH)


def lanes(i, width):
    return pl.ds(pl.multiple_of(i * width, width), width)


class Ring:
    def __init__(self, links, count, z, ch):
        self.links, self.count, self.z, self.ch = links, count, z, ch
        self.far = count // 2

    def at(self, way, k):
        return lax.rem(self.z + (1 - 2 * way) * k + 2 * self.count, self.count)

    def next(self, way):
        return (self.at(way, 1), self.ch)

    def hops(self, way, lot):
        return self.far if lot % 2 == way else self.count - 1 - self.far

    def came(self, here, sems, way, lot, step):
        self.links.copy(
            here, here, sems[0].at[way, lot, step], sems[1].at[way, lot, step], self.next(way)
        ).wait_recv()

    def go(self, src, dst, sems, way, lot, step):
        self.links.send(
            src, dst, sems[0].at[way, lot, step], sems[1].at[way, lot, step], self.next(way)
        )

    def spread(self, region, lots, sems):
        for step in range(self.far + 1):
            for lot in range(lots):
                for way in range(2):
                    n = self.hops(way, lot)
                    if step > n:
                        continue
                    here = region(self.at(way, -step), lot)
                    if step > 0:
                        self.came(here, sems, way, lot, step - 1)
                    if step < n:
                        self.go(here, here, sems, way, lot, step)
            yield

    def reduce(self, term, slot, lots, sems, keep):
        for step in range(self.far):
            for lot in range(lots):
                for way in range(2):
                    n = self.hops(way, lot)
                    if step >= n:
                        continue
                    here = slot(way, lot, step)
                    value = term(self.at(way, n - step), lot)
                    if step > 0:
                        self.came(here, sems, way, lot, step - 1)
                        value = value + here[...].astype(f32)
                    here[...] = value.astype(bf16)
                    self.go(here, slot(way, lot, step + 1), sems, way, lot, step)
            yield
        for lot in range(lots):
            value = term(self.z, lot)
            for way in range(2):
                n = self.hops(way, lot)
                here = slot(way, lot, n)
                self.came(here, sems, way, lot, n - 1)
                value = value + here[...].astype(f32)
            keep(lot, value)


def kernel(
    count, lengths, q_in, key_in, val_in, w, d_out, rate_in, res_in, skip_in,
    out, dq, dk, dv, small, dw,
    q, key, val, rate_ref, res_ref, skip, dq_own, dk_own, dv_own,
    G, H, W2, WC, xs, gs, ys, hs, field, dp, dp_send, prod, out_send, out_all,
    states, state_got, small_all, small_sum, dw_own, dw_send, dw_got, ring_buf, dw_all,
    g_send, g_recv, h_send, h_recv, loc, one_s, one_r, a2a_s, a2a_r, wz_s, wz_r,
    st_s, st_r, sm_s, sm_r, rs_s, rs_r, ag_s, ag_r, acc_ref, dw_sem,
):
    z, ch = lax.axis_index("pos"), lax.axis_index("ch")
    core, chip = lax.rem(ch, 2), lax.div(ch, 2)
    x, y = lax.div(chip, SIDE), lax.rem(chip, SIDE)
    mate = (z, chip * 2 + 1 - core)
    other = 1 - core
    t, c = q.shape
    half = t // 2
    wide = 2 * c
    n_out = w.shape[1]

    def along(k):
        return (lax.rem(z + k + count, count), ch)

    def chip_at(k):
        return lax.rem(chip + k, CHIPS)

    barrier = pltpu.get_barrier_semaphore()
    peers = [mate] + [along(k) for k in range(1, count)]
    peers += [(z, chip_at(k) * 2 + core) for k in range(1, CHIPS)]
    for device in peers:
        pl.semaphore_signal(barrier, inc=1, device_id=device, device_id_type=MESH)

    mine, its = lanes(core, half), lanes(other, half)
    own_cols = pl.ds(pl.multiple_of(chip * wide + core * c, c), c)
    mate_cols = pl.ds(pl.multiple_of(chip * wide + other * c, c), c)
    slab = c // count
    own_rows = pl.ds(pl.multiple_of(z * slab, slab), slab)
    slab_rows = pl.ds(pl.multiple_of(core * c + z * slab, slab), slab)
    local = [
        pltpu.make_async_copy(src, dst, loc.at[n])
        for n, (src, dst) in enumerate(
            [
                (d_out.at[mine], G.at[:, own_cols]),
                (key_in, key),
                (val_in, val),
                (rate_in, rate_ref),
                (res_in, res_ref),
                (skip_in, skip),
                (q_in, q),
                (w.at[own_rows, lanes(chip, wide)], WC.at[chip, slab_rows]),
                (w, W2.at[lanes(core, c)]),
            ]
        )
    ]
    for copy in local:
        copy.start()
    pl.semaphore_wait(barrier, len(peers))

    links = Links()
    links.send(d_out.at[its], G.at[:, own_cols], one_s.at[0], one_r.at[0], mate)
    for k in range(1, CHIPS):
        links.send(
            w.at[own_rows, lanes(chip_at(k), wide)], WC.at[chip, slab_rows],
            a2a_s.at[k], a2a_r.at[k], (z, chip_at(k) * 2 + core),
        )

    def got_one(ref, i):
        links.copy(ref, ref, one_s.at[i], one_r.at[i], mate).wait_recv()

    for n in range(1, 6):
        local[n].wait()
    rate, residue = rate_ref[...], res_ref[...]
    xx = key[...].astype(f32) * val[...].astype(f32)
    interleave(xs, xx)
    local[0].wait()
    got_one(G.at[:, mate_cols], 0)
    first = Gather(links, G, g_send, g_recv, z, x, y, core)
    first.wave(0)
    sub = t // NSUB
    p = scan_states(xs, rate, False)
    states[0] = edge_of(p, False)
    for n in (1, 2, 3):
        links.send(
            states.at[0], state_got.at[0, n - 1], st_s.at[0, n - 1], st_r.at[0, n - 1], along(n)
        )
    links.send(w, W2.at[lanes(core, c)], one_s.at[1], one_r.at[1], mate)

    def document(b):
        end, before = lengths[0], jnp.int32(0)
        for n in range(lengths.shape[0]):
            before = before + jnp.where(end <= b, 1, 0)
            if n + 1 < lengths.shape[0]:
                end = end + lengths[n + 1]
        return before

    def carried(way):
        total = None
        for n in (1, 2, 3):
            here = state_got.at[way, n - 1]
            links.copy(here, here, st_s.at[way, n - 1], st_r.at[way, n - 1], mate).wait_recv()
            b = z + n if way else z - n
            same = (b >= 0) & (b < count) & (document(b) == document(z))
            decay = jnp.exp(-rate * float(t * (n - 1))) * jnp.where(same, 1.0, 0.0).astype(f32)
            term = decay * here[...]
            total = term if total is None else total + term
        return total

    start = entering_of(p, rate, sub, carried(0), False)
    forward_pass(xs, ys, hs, rate, residue, start)
    first.wave(1)
    cc = deinterleave(ys) + skip[...] * xx
    field[...] = cc
    local[6].wait()
    prod[...] = (q[...].astype(f32) * cc).astype(bf16)
    links.send(prod.at[its], H.at[:, own_cols], one_s.at[2], one_r.at[2], mate)
    H[:, own_cols] = prod[mine, :]
    ring = Ring(links, count, z, ch)
    lot_chips = CHIPS // 2

    def columns(s, lot):
        rows = pl.ds(pl.multiple_of(core * c + s * slab, slab), slab)
        return WC.at[lot * lot_chips : (lot + 1) * lot_chips, rows]

    got_one(H.at[:, mate_cols], 2)
    second = Gather(links, H, h_send, h_recv, z, x, y, core)

    def chip_of(p):
        i, j = OFFSETS[p]
        return lax.rem(x + i + SIDE, SIDE) * SIDE + lax.rem(y + j + SIDE, SIDE)

    both = jnp.concatenate([H[:, mate_cols].T, H[:, own_cols].T], axis=0)

    def packed(first_one, last):
        return pl.ds(first_one * wide, (last - first_one) * wide)

    def weight_part(group):
        lots = GROUPS[group]
        for p in range(lots[0][0], lots[-1][1]):
            r = jnp.dot(both, G[:, lanes(chip_of(p), wide)], preferred_element_type=f32)
            dw_send[:, packed(p, p + 1)] = r[:c].astype(bf16)
            dw_own[:, packed(p, p + 1)] = r[c:]
        cols = packed(lots[0][0], lots[-1][1])
        links.send(
            dw_send.at[:, cols], dw_got.at[:, cols], one_s.at[7 + group], one_r.at[7 + group], mate
        )

    def sums(group):
        lots = GROUPS[group]
        cols = packed(lots[0][0], lots[-1][1])
        got_one(dw_got.at[:, cols], 7 + group)

        def term(s, lot):
            rows, part = lanes(s, slab), packed(*lots[lot])
            return dw_own[rows, part] + dw_got[rows, part].astype(f32)

        def slot(way, lot, step):
            return ring_buf.at[
                group, way, lot, step, :, pl.ds(0, (lots[lot][1] - lots[lot][0]) * wide)
            ]

        def keep(lot, value):
            dw_all[lanes(z, slab), packed(*lots[lot])] = value.astype(bf16)

        def block_of(s, lot):
            return dw_all.at[lanes(s, slab), packed(*lots[lot])]

        yield from ring.reduce(term, slot, 2, (rs_s.at[group], rs_r.at[group]), keep)
        yield from ring.spread(block_of, 2, (ag_s.at[group], ag_r.at[group]))
        for p in range(lots[0][0], lots[-1][1]):
            copy = pltpu.make_async_copy(
                dw_all.at[:, packed(p, p + 1)], dw.at[:, lanes(chip_of(p), wide)], dw_sem.at[p]
            )
            copy.start()
            done.append(copy)

    done = []

    def weight_columns():
        local[7].wait()
        for k in range(1, CHIPS):
            here = WC.at[chip_at(CHIPS - k), slab_rows]
            links.copy(here, here, a2a_s.at[k], a2a_r.at[k], mate).wait_recv()
        yield from ring.spread(columns, 2, (wz_s, wz_r))
        links.send(
            WC.at[:, lanes(core, c)], WC.at[:, lanes(core, c)], one_s.at[5], one_r.at[5], mate
        )

    rounds = {"w": weight_columns(), "0": sums(0), "1": sums(1), "2": sums(2)}

    def product_part(lo, hi, acc):
        for p in range(lo, hi):
            cols = lanes(chip_of(p), wide)
            part = lax.dot_general(
                G[:, cols], W2[:, cols], (((1,), (1,)), ((), ())), preferred_element_type=f32
            )
            acc = part if acc is None else acc + part
        return acc

    def out_part(lo, hi, acc):
        for p in range(lo, hi):
            part = jnp.dot(
                H[:, lanes(chip_of(p), wide)], WC[chip_of(p)], preferred_element_type=f32
            )
            acc = part if acc is None else acc + part
        return acc

    near = GROUPS[1][-1][1]
    is_first = core == 0

    def product_near():
        local[8].wait()
        got_one(W2.at[lanes(other, c)], 1)
        acc_ref[...] = product_part(0, near, None)

    def product_far():
        acc = product_part(near, CHIPS, acc_ref[...])
        dp[mine, :] = jnp.where(is_first, acc[:, :c], acc[:, c:])
        dp_send[...] = jnp.where(is_first, acc[:, c:], acc[:, :c])
        links.send(dp_send, dp.at[mine], one_s.at[3], one_r.at[3], mate)

    kept = {}

    def back_states():
        got_one(dp.at[its], 3)
        g = dp[...] * q[...].astype(f32)
        interleave(gs, g)
        kept["g"] = g
        kept["p"] = scan_states(gs, rate, True)
        states[1] = edge_of(kept["p"], True)
        for n in (1, 2, 3):
            links.send(
                states.at[1], state_got.at[1, n - 1], st_s.at[1, n - 1], st_r.at[1, n - 1], along(-n)
            )

    def back_start():
        start = entering_of(kept["p"], rate, sub, carried(1), True)
        kept["sums"] = []
        kept["back"] = backward_pieces(xs, gs, ys, hs, rate, residue, start, 2, kept["sums"])

    def back_piece():
        next(kept["back"], None)

    def back_end():
        g, result = kept["g"], kept["sums"]
        dskip = jnp.sum(xx * g, axis=0, keepdims=True)
        for n in range(2):
            small_all[z, n * GROUP : (n + 1) * GROUP] = result[n]
            small_all[z, MODES + n * GROUP : MODES + (n + 1) * GROUP] = result[2 + n]
        small_all[z, 2 * MODES :] = jnp.broadcast_to(dskip, (GROUP, c))
        for n in range(1, count):
            links.send(small_all.at[z], small_all.at[z], sm_s.at[n], sm_r.at[n], along(n))
        dq_own[...] = (dp[...] * field[...]).astype(bf16)
        dm = deinterleave(ys) + skip[...] * g
        dk_own[...] = (dm * val[...].astype(f32)).astype(bf16)
        dv_own[...] = (dm * key[...].astype(f32)).astype(bf16)
        for n, (src, dst) in enumerate([(dq_own, dq), (dk_own, dk), (dv_own, dv)]):
            copy = pltpu.make_async_copy(src, dst, loc.at[n])
            copy.start()
            done.append(copy)

    def out_near():
        for _ in rounds["w"]:
            pass
        got_one(WC.at[:, lanes(other, c)], 5)
        acc_ref[...] = out_part(0, near, None)

    def out_far():
        acc = out_part(near, CHIPS, acc_ref[...])
        out_all[mine, :] = jnp.where(is_first, acc[:, :c], acc[:, c:]).astype(bf16)
        out_send[...] = jnp.where(is_first, acc[:, c:], acc[:, :c]).astype(bf16)
        links.send(out_send, out_all.at[mine], one_s.at[6], one_r.at[6], mate)

    tasks = {
        "p0": product_near, "p1": product_far, "bs": back_states, "be": back_start,
        "b": back_piece, "bz": back_end, "o0": out_near, "o1": out_far,
    }
    for name in SCHEDULE:
        if name in tasks:
            tasks[name]()
        elif name[0] == "g":
            weight_part(int(name[1]))
        elif name[0] == "f":
            first.wave(int(name[1]))
        elif name[0] == "s":
            second.wave(int(name[1]))
        else:
            for one in name[1:]:
                next(rounds[one], None)
    for one in rounds.values():
        for _ in one:
            pass
    for n in range(1, count):
        here = small_all.at[ring.at(0, -n)]
        links.copy(here, here, sm_s.at[n], sm_r.at[n], mate).wait_recv()
    total = small_all[0]
    for n in range(1, count):
        total = total + small_all[n]
    small_sum[...] = total
    got_one(out_all.at[its], 6)
    for n, (src, dst) in enumerate([(small_sum, small), (out_all, out)]):
        copy = pltpu.make_async_copy(src, dst, loc.at[3 + n])
        copy.start()
        done.append(copy)
    links.drain()
    for copy in done:
        copy.wait()


def finish(out_in, dq_in, dk_in, dv_in, small, dw_in, out, dq, dk, dv, dres, drate, dskip, dw):
    out[...] = out_in[...]
    dq[...] = dq_in[...]
    dk[...] = dk_in[...]
    dv[...] = dv_in[...]
    dres[...] = small[:MODES]
    drate[...] = small[MODES : 2 * MODES]
    dskip[...] = small[2 * MODES : 2 * MODES + 1]
    dw[...] = dw_in[...].astype(f32)


def shards(queries, keys, values, residue, rate, skip, w_out, lengths, d_out):
    t, c = queries.shape
    n_out = w_out.shape[1]
    count = lax.axis_size("pos")
    thin = jax.ShapeDtypeStruct((t, c), bf16)
    rows = 2 * MODES + GROUP
    vmem, dma = pltpu.VMEM, pltpu.SemaphoreType.DMA
    wide, half, far = 2 * c, t // 2, count // 2
    tall, short = vmem((t, c), f32), vmem((t, c), bf16)
    few = vmem((MODES, c), f32)
    scratch = [
        short, short, short, few, few, vmem((1, c), f32), short, short, short,
        vmem((half, n_out), bf16), vmem((half, n_out), bf16), vmem((wide, n_out), bf16),
        vmem((CHIPS, wide, wide), bf16), tall, tall, tall,
        vmem((t // NSUB, MODES, NSUB, c), f32), tall, tall, vmem((half, c), f32),
        short, vmem((half, c), bf16), short,
        vmem((2, MODES, c), f32), vmem((2, 3, MODES, c), f32), vmem((count, rows, c), f32),
        vmem((rows, c), f32),
        vmem((c, n_out), f32), vmem((c, n_out), bf16), vmem((c, n_out), bf16),
        vmem((3, 2, 2, far + 1, c // count, 3 * wide), bf16), vmem((c, n_out), bf16),
        dma((2, len(KEYS))), dma((2, len(KEYS))), dma((2, len(KEYS))), dma((2, len(KEYS))),
        dma((9,)), dma((10,)), dma((10,)), dma((CHIPS,)), dma((CHIPS,)),
        dma((2, 2, far)), dma((2, 2, far)), dma((2, 3)), dma((2, 3)), dma((count,)), dma((count,)),
        dma((3, 2, 2, far)), dma((3, 2, 2, far)), dma((3, 2, 2, far)), dma((3, 2, 2, far)),
        vmem((half, wide), f32), dma((CHIPS,)),
    ]
    whole = pl.BlockSpec(memory_space=pltpu.VMEM)
    apart = pl.BlockSpec(memory_space=pl.ANY)
    out, dq, dk, dv, small, dw = pl.pallas_call(
        functools.partial(kernel, count),
        out_shape=(
            thin, thin, thin, thin, jax.ShapeDtypeStruct((rows, c), f32),
            jax.ShapeDtypeStruct((c, n_out), bf16),
        ),
        in_specs=[pl.BlockSpec(memory_space=pltpu.SMEM)] + [apart] * 8,
        out_specs=(apart,) * 6,
        scratch_shapes=scratch,
        compiler_params=pltpu.CompilerParams(
            collective_id=0, has_side_effects=True, vmem_limit_bytes=60 * MIB
        ),
    )(lengths, queries, keys, values, w_out, d_out, rate.T, residue.T, skip[None, :])
    state = jax.ShapeDtypeStruct((MODES, c), f32)
    out, dq, dk, dv, dres, drate, dskip, dw = pl.pallas_call(
        finish,
        out_shape=(
            thin, thin, thin, thin, state, state, jax.ShapeDtypeStruct((1, c), f32),
            jax.ShapeDtypeStruct((c, n_out), f32),
        ),
        in_specs=[whole] * 6,
        out_specs=(whole,) * 8,
        compiler_params=pltpu.CompilerParams(vmem_limit_bytes=60 * MIB),
    )(out, dq, dk, dv, small, dw)
    return out, dq, dk, dv, dres.T, drate.T, dskip[0], dw


def solution(mesh):
    both, chan = P("pos", "ch"), P("ch", None)
    return jax.shard_map(
        shards,
        mesh=mesh,
        in_specs=(both, both, both, chan, chan, P("ch"), chan, P(), both),
        out_specs=(both, both, both, both, chan, chan, P("ch"), chan),
        check_vma=False,
    )
```

```python
import functools

import jax
import jax.numpy as jnp
from jax import lax
from jax.experimental import pallas as pl
from jax.experimental.pallas import tpu as pltpu
from jax.sharding import PartitionSpec as P

f32 = jnp.float32
bf16 = jnp.bfloat16
MODES = 16
GROUP = 8
NSUB = 8
UNROLL = 4
SIDE = 4
CHIPS = SIDE * SIDE
MESH = pl.DeviceIdType.MESH
MIB = 1024 * 1024


def rows_of(s):
    return pl.ds(pl.multiple_of(s * NSUB, NSUB), NSUB)


def interleave(dst, val):
    sub = val.shape[0] // NSUB
    for n in range(NSUB):
        dst[pl.ds(n, sub, stride=NSUB), :] = val[n * sub : (n + 1) * sub]


def deinterleave(src):
    sub = src.shape[0] // NSUB
    return jnp.concatenate([src[pl.ds(n, sub, stride=NSUB), :] for n in range(NSUB)], axis=0)


def spread(a):
    return jnp.broadcast_to(a[:, None, :], (a.shape[0], NSUB, a.shape[1]))


def place_of(shape):
    return lax.broadcasted_iota(jnp.int32, shape, 1)


def scan_states(src, rate, reverse):
    sub = src.shape[0] // NSUB
    lam = spread(jnp.exp(-rate))

    def step(i, h):
        s = sub - 1 - i if reverse else i
        return lam * h + src[rows_of(s), :][None]

    p = lax.fori_loop(0, sub, step, jnp.zeros_like(lam), unroll=UNROLL)
    place = place_of(p.shape)
    for k in (1, 2, 4):
        moved = pltpu.roll(p, NSUB - k if reverse else k, 1)
        ok = place < NSUB - k if reverse else place >= k
        p = p + spread(jnp.exp(-rate * (sub * k))) * jnp.where(ok, moved, 0.0)
    return p


def edge_of(p, reverse):
    return jnp.sum(jnp.where(place_of(p.shape) == (0 if reverse else NSUB - 1), p, 0.0), axis=1)


def entering_of(p, rate, sub, carry, reverse):
    place = place_of(p.shape)
    moved = pltpu.roll(p, NSUB - 1 if reverse else 1, 1)
    ok = place < NSUB - 1 if reverse else place >= 1
    steps = (NSUB - 1 - place if reverse else place).astype(f32) * float(sub)
    return jnp.where(ok, moved, 0.0) + jnp.exp(-spread(rate) * steps) * spread(carry)


def forward_pass(xs, ys, hs, rate, residue, start):
    sub = xs.shape[0] // NSUB
    for lo in range(0, MODES, GROUP):
        part = slice(lo, lo + GROUP)
        lam, res = spread(jnp.exp(-rate[part])), spread(residue[part])

        def step(s, h):
            hs[s, part] = h
            h = lam * h + xs[rows_of(s), :][None]
            y = jnp.sum(res * h, axis=0)
            ys[rows_of(s), :] = y if lo == 0 else ys[rows_of(s), :] + y
            return h

        lax.fori_loop(0, sub, step, start[part], unroll=UNROLL)


def backward_pieces(xs, gs, ms, hs, rate, residue, start, pieces, result):
    sub = xs.shape[0] // NSUB
    span = sub // pieces
    d_res, d_rate = [], []
    for lo in range(0, MODES, GROUP):
        part = slice(lo, lo + GROUP)
        lam, res = spread(jnp.exp(-rate[part])), spread(residue[part])

        def step(i, carry):
            a, dr, dt = carry
            s = sub - 1 - i
            a = lam * a + gs[rows_of(s), :][None]
            m = jnp.sum(res * a, axis=0)
            ms[rows_of(s), :] = m if lo == 0 else ms[rows_of(s), :] + m
            return a, dr + a * xs[rows_of(s), :][None], dt + a * hs[s, part]

        zero = jnp.zeros_like(lam)
        carry = (start[part], zero, zero)
        for piece in range(pieces):
            carry = lax.fori_loop(piece * span, (piece + 1) * span, step, carry, unroll=UNROLL)
            yield
        d_res.append(jnp.sum(carry[1], axis=1))
        d_rate.append(-residue[part] * jnp.exp(-rate[part]) * jnp.sum(carry[2], axis=1))
    result.extend(d_res + d_rate)


class Links:
    def __init__(self):
        self.sent = []

    def copy(self, src, dst, send, recv, device):
        return pltpu.make_async_remote_copy(
            src_ref=src, dst_ref=dst, send_sem=send, recv_sem=recv,
            device_id=device, device_id_type=MESH,
        )

    def send(self, *args):
        c = self.copy(*args)
        c.start()
        self.sent.append(c)

    def drain(self):
        for c in self.sent:
            c.wait_send()
        self.sent = []


NEAR = (-1, 0, 1, 2)
FULL, LOW, HIGH = range(3)
KEYS = [(1, 0, FULL), (-1, 0, FULL), (2, 0, LOW), (2, 0, HIGH)]
for i in (0, 1, -1, 2):
    KEYS += [(i, 1, FULL), (i, -1, FULL), (i, 2, LOW), (i, 2, HIGH)]
OFFSETS = sorted([(i, j) for i in NEAR for j in NEAR], key=lambda o: abs(o[0]) + abs(o[1]))
SCHEDULE = (
    "tw", "g0", "f2", "t0w", "g1", "p0", "f3", "t01w", "s0", "f4", "g2", "t012w", "p1", "bs",
    "t012w", "s1", "be", "t012w", "b", "b", "t012w", "b", "b", "t012", "s2", "b", "bz", "t012",
    "t012", "s3", "t012", "o0", "t012", "s4", "t012", "o1",
)
GROUPS = [((0, 3), (3, 5)), ((5, 8), (8, 11)), ((11, 13), (13, 16))]


class Gather:
    def __init__(self, links, buf, send, recv, z, x, y, core):
        self.links, self.buf, self.send_sem, self.recv_sem = links, buf, send, recv
        self.z, self.at, self.core = z, (x, y), core

    def region(self, kind, i, j, part):
        at = list(self.at)
        at[kind] = lax.rem(at[kind] + i + SIDE, SIDE)
        at[1 - kind] = lax.rem(at[1 - kind] + j + SIDE, SIDE)
        rows = self.buf.shape[0] // 2
        start = kind * rows + (rows // 2 if part == HIGH else 0)
        wide = self.buf.shape[1] // CHIPS
        return self.buf.at[
            pl.ds(start, rows if part == FULL else rows // 2), lanes(at[0] * SIDE + at[1], wide)
        ]

    def device(self, axis, sign):
        at = list(self.at)
        at[axis] = lax.rem(at[axis] + sign + SIDE, SIDE)
        return (self.z, (at[0] * SIDE + at[1]) * 2 + self.core)

    def send(self, kind, i, j, part):
        n = KEYS.index((i, j, part))
        step = {LOW: 1, HIGH: -1}.get(part, 0)
        away = j if j else i
        sign = -step if step else -away
        here = self.region(kind, i, step, part) if j else self.region(kind, step, 0, part)
        self.links.send(
            here, here, self.send_sem.at[kind, n], self.recv_sem.at[kind, n],
            self.device(1 - kind if j else kind, sign),
        )

    def got(self, kind, i, j, part):
        n = KEYS.index((i, j, part))
        here = self.region(kind, i, j, part)
        self.links.copy(
            here, here, self.send_sem.at[kind, n], self.recv_sem.at[kind, n], self.device(kind, 1)
        ).wait_recv()

    def wave(self, k):
        for i in (1, -1, 2, 0):
            for j in (0, 1, -1, 2):
                if abs(i) + abs(j) != k:
                    continue
                for kind in range(2):
                    for part in (LOW, HIGH) if 2 in (i, j) and (j == 2 or j == 0) else (FULL,):
                        if k > 0:
                            self.got(kind, i, j, part)
                    if k == 0:
                        self.send(kind, 1, 0, FULL)
                        self.send(kind, -1, 0, FULL)
                    elif j == 0 and abs(i) == 1:
                        self.send(kind, 2, 0, LOW if i == 1 else HIGH)
                    if j == 0:
                        self.send(kind, i, 1, FULL)
                        self.send(kind, i, -1, FULL)
                    elif abs(j) == 1:
                        self.send(kind, i, 2, LOW if j == 1 else HIGH)


def lanes(i, width):
    return pl.ds(pl.multiple_of(i * width, width), width)


class Ring:
    def __init__(self, links, count, z, ch):
        self.links, self.count, self.z, self.ch = links, count, z, ch
        self.far = count // 2

    def at(self, way, k):
        return lax.rem(self.z + (1 - 2 * way) * k + 2 * self.count, self.count)

    def next(self, way):
        return (self.at(way, 1), self.ch)

    def hops(self, way, lot):
        return self.far if lot % 2 == way else self.count - 1 - self.far

    def came(self, here, sems, way, lot, step):
        self.links.copy(
            here, here, sems[0].at[way, lot, step], sems[1].at[way, lot, step], self.next(way)
        ).wait_recv()

    def go(self, src, dst, sems, way, lot, step):
        self.links.send(
            src, dst, sems[0].at[way, lot, step], sems[1].at[way, lot, step], self.next(way)
        )

    def spread(self, region, lots, sems):
        for step in range(self.far + 1):
            for lot in range(lots):
                for way in range(2):
                    n = self.hops(way, lot)
                    if step > n:
                        continue
                    here = region(self.at(way, -step), lot)
                    if step > 0:
                        self.came(here, sems, way, lot, step - 1)
                    if step < n:
                        self.go(here, here, sems, way, lot, step)
            yield

    def reduce(self, term, slot, lots, sems, keep):
        for step in range(self.far):
            for lot in range(lots):
                for way in range(2):
                    n = self.hops(way, lot)
                    if step >= n:
                        continue
                    here = slot(way, lot, step)
                    value = term(self.at(way, n - step), lot)
                    if step > 0:
                        self.came(here, sems, way, lot, step - 1)
                        value = value + here[...].astype(f32)
                    here[...] = value.astype(bf16)
                    self.go(here, slot(way, lot, step + 1), sems, way, lot, step)
            yield
        for lot in range(lots):
            value = term(self.z, lot)
            for way in range(2):
                n = self.hops(way, lot)
                here = slot(way, lot, n)
                self.came(here, sems, way, lot, n - 1)
                value = value + here[...].astype(f32)
            keep(lot, value)


def kernel(
    count, lengths, q_in, key_in, val_in, w, d_out, rate_in, res_in, skip_in,
    out, dq, dk, dv, small, dw,
    q, key, val, rate_ref, res_ref, skip, dq_own, dk_own, dv_own,
    G, H, W2, WC, xs, gs, ys, hs, field, dp, dp_send, prod, out_send, out_all,
    states, state_got, small_all, small_sum, dw_own, dw_send, dw_got, ring_buf, dw_all,
    g_send, g_recv, h_send, h_recv, loc, one_s, one_r, a2a_s, a2a_r, wz_s, wz_r,
    st_s, st_r, sm_s, sm_r, rs_s, rs_r, ag_s, ag_r, acc_ref, dw_sem,
):
    z, ch = lax.axis_index("pos"), lax.axis_index("ch")
    core, chip = lax.rem(ch, 2), lax.div(ch, 2)
    x, y = lax.div(chip, SIDE), lax.rem(chip, SIDE)
    mate = (z, chip * 2 + 1 - core)
    other = 1 - core
    t, c = q.shape
    half = t // 2
    wide = 2 * c
    n_out = w.shape[1]

    def along(k):
        return (lax.rem(z + k + count, count), ch)

    def chip_at(k):
        return lax.rem(chip + k, CHIPS)

    barrier = pltpu.get_barrier_semaphore()
    peers = [mate] + [along(k) for k in range(1, count)]
    peers += [(z, chip_at(k) * 2 + core) for k in range(1, CHIPS)]
    for device in peers:
        pl.semaphore_signal(barrier, inc=1, device_id=device, device_id_type=MESH)

    mine, its = lanes(core, half), lanes(other, half)
    own_cols = pl.ds(pl.multiple_of(chip * wide + core * c, c), c)
    mate_cols = pl.ds(pl.multiple_of(chip * wide + other * c, c), c)
    slab = c // count
    own_rows = pl.ds(pl.multiple_of(z * slab, slab), slab)
    slab_rows = pl.ds(pl.multiple_of(core * c + z * slab, slab), slab)
    local = [
        pltpu.make_async_copy(src, dst, loc.at[n])
        for n, (src, dst) in enumerate(
            [
                (d_out.at[mine], G.at[:, own_cols]),
                (key_in, key),
                (val_in, val),
                (rate_in, rate_ref),
                (res_in, res_ref),
                (skip_in, skip),
                (q_in, q),
                (w.at[own_rows, lanes(chip, wide)], WC.at[chip, slab_rows]),
                (w, W2.at[lanes(core, c)]),
            ]
        )
    ]
    for copy in local:
        copy.start()
    pl.semaphore_wait(barrier, len(peers))

    links = Links()
    links.send(d_out.at[its], G.at[:, own_cols], one_s.at[0], one_r.at[0], mate)
    for k in range(1, CHIPS):
        links.send(
            w.at[own_rows, lanes(chip_at(k), wide)], WC.at[chip, slab_rows],
            a2a_s.at[k], a2a_r.at[k], (z, chip_at(k) * 2 + core),
        )

    def got_one(ref, i):
        links.copy(ref, ref, one_s.at[i], one_r.at[i], mate).wait_recv()

    for n in range(1, 6):
        local[n].wait()
    rate, residue = rate_ref[...], res_ref[...]
    xx = key[...].astype(f32) * val[...].astype(f32)
    interleave(xs, xx)
    local[0].wait()
    got_one(G.at[:, mate_cols], 0)
    first = Gather(links, G, g_send, g_recv, z, x, y, core)
    first.wave(0)
    sub = t // NSUB
    p = scan_states(xs, rate, False)
    states[0] = edge_of(p, False)
    for n in (1, 2, 3):
        links.send(
            states.at[0], state_got.at[0, n - 1], st_s.at[0, n - 1], st_r.at[0, n - 1], along(n)
        )
    links.send(w, W2.at[lanes(core, c)], one_s.at[1], one_r.at[1], mate)

    def document(b):
        end, before = lengths[0], jnp.int32(0)
        for n in range(lengths.shape[0]):
            before = before + jnp.where(end <= b, 1, 0)
            if n + 1 < lengths.shape[0]:
                end = end + lengths[n + 1]
        return before

    def carried(way):
        total = None
        for n in (1, 2, 3):
            here = state_got.at[way, n - 1]
            links.copy(here, here, st_s.at[way, n - 1], st_r.at[way, n - 1], mate).wait_recv()
            b = z + n if way else z - n
            same = (b >= 0) & (b < count) & (document(b) == document(z))
            decay = jnp.exp(-rate * float(t * (n - 1))) * jnp.where(same, 1.0, 0.0).astype(f32)
            term = decay * here[...]
            total = term if total is None else total + term
        return total

    start = entering_of(p, rate, sub, carried(0), False)
    forward_pass(xs, ys, hs, rate, residue, start)
    first.wave(1)
    cc = deinterleave(ys) + skip[...] * xx
    field[...] = cc
    local[6].wait()
    prod[...] = (q[...].astype(f32) * cc).astype(bf16)
    links.send(prod.at[its], H.at[:, own_cols], one_s.at[2], one_r.at[2], mate)
    H[:, own_cols] = prod[mine, :]
    ring = Ring(links, count, z, ch)
    lot_chips = CHIPS // 2

    def columns(s, lot):
        rows = pl.ds(pl.multiple_of(core * c + s * slab, slab), slab)
        return WC.at[lot * lot_chips : (lot + 1) * lot_chips, rows]

    got_one(H.at[:, mate_cols], 2)
    second = Gather(links, H, h_send, h_recv, z, x, y, core)

    def chip_of(p):
        i, j = OFFSETS[p]
        return lax.rem(x + i + SIDE, SIDE) * SIDE + lax.rem(y + j + SIDE, SIDE)

    both = jnp.concatenate([H[:, mate_cols].T, H[:, own_cols].T], axis=0)

    def packed(first_one, last):
        return pl.ds(first_one * wide, (last - first_one) * wide)

    def weight_part(group):
        lots = GROUPS[group]
        for p in range(lots[0][0], lots[-1][1]):
            r = jnp.dot(both, G[:, lanes(chip_of(p), wide)], preferred_element_type=f32)
            dw_send[:, packed(p, p + 1)] = r[:c].astype(bf16)
            dw_own[:, packed(p, p + 1)] = r[c:]
        cols = packed(lots[0][0], lots[-1][1])
        links.send(
            dw_send.at[:, cols], dw_got.at[:, cols], one_s.at[7 + group], one_r.at[7 + group], mate
        )

    def sums(group):
        lots = GROUPS[group]
        cols = packed(lots[0][0], lots[-1][1])
        got_one(dw_got.at[:, cols], 7 + group)

        def term(s, lot):
            rows, part = lanes(s, slab), packed(*lots[lot])
            return dw_own[rows, part] + dw_got[rows, part].astype(f32)

        def slot(way, lot, step):
            return ring_buf.at[
                group, way, lot, step, :, pl.ds(0, (lots[lot][1] - lots[lot][0]) * wide)
            ]

        def keep(lot, value):
            dw_all[lanes(z, slab), packed(*lots[lot])] = value.astype(bf16)

        def block_of(s, lot):
            return dw_all.at[lanes(s, slab), packed(*lots[lot])]

        yield from ring.reduce(term, slot, 2, (rs_s.at[group], rs_r.at[group]), keep)
        yield from ring.spread(block_of, 2, (ag_s.at[group], ag_r.at[group]))
        for p in range(lots[0][0], lots[-1][1]):
            copy = pltpu.make_async_copy(
                dw_all.at[:, packed(p, p + 1)], dw.at[:, lanes(chip_of(p), wide)], dw_sem.at[p]
            )
            copy.start()
            done.append(copy)

    done = []

    def weight_columns():
        local[7].wait()
        for k in range(1, CHIPS):
            here = WC.at[chip_at(CHIPS - k), slab_rows]
            links.copy(here, here, a2a_s.at[k], a2a_r.at[k], mate).wait_recv()
        yield from ring.spread(columns, 2, (wz_s, wz_r))
        links.send(
            WC.at[:, lanes(core, c)], WC.at[:, lanes(core, c)], one_s.at[5], one_r.at[5], mate
        )

    rounds = {"w": weight_columns(), "0": sums(0), "1": sums(1), "2": sums(2)}

    def product_part(lo, hi, acc):
        for p in range(lo, hi):
            cols = lanes(chip_of(p), wide)
            part = lax.dot_general(
                G[:, cols], W2[:, cols], (((1,), (1,)), ((), ())), preferred_element_type=f32
            )
            acc = part if acc is None else acc + part
        return acc

    def out_part(lo, hi, acc):
        for p in range(lo, hi):
            part = jnp.dot(
                H[:, lanes(chip_of(p), wide)], WC[chip_of(p)], preferred_element_type=f32
            )
            acc = part if acc is None else acc + part
        return acc

    near = GROUPS[1][-1][1]
    is_first = core == 0

    def product_near():
        local[8].wait()
        got_one(W2.at[lanes(other, c)], 1)
        acc_ref[...] = product_part(0, near, None)

    def product_far():
        acc = product_part(near, CHIPS, acc_ref[...])
        dp[mine, :] = jnp.where(is_first, acc[:, :c], acc[:, c:])
        dp_send[...] = jnp.where(is_first, acc[:, c:], acc[:, :c])
        links.send(dp_send, dp.at[mine], one_s.at[3], one_r.at[3], mate)

    kept = {}

    def back_states():
        got_one(dp.at[its], 3)
        g = dp[...] * q[...].astype(f32)
        interleave(gs, g)
        kept["g"] = g
        kept["p"] = scan_states(gs, rate, True)
        states[1] = edge_of(kept["p"], True)
        for n in (1, 2, 3):
            links.send(
                states.at[1], state_got.at[1, n - 1], st_s.at[1, n - 1], st_r.at[1, n - 1], along(-n)
            )

    def back_start():
        start = entering_of(kept["p"], rate, sub, carried(1), True)
        kept["sums"] = []
        kept["back"] = backward_pieces(xs, gs, ys, hs, rate, residue, start, 2, kept["sums"])

    def back_piece():
        next(kept["back"], None)

    def back_end():
        g, result = kept["g"], kept["sums"]
        dskip = jnp.sum(xx * g, axis=0, keepdims=True)
        for n in range(2):
            small_all[z, n * GROUP : (n + 1) * GROUP] = result[n]
            small_all[z, MODES + n * GROUP : MODES + (n + 1) * GROUP] = result[2 + n]
        small_all[z, 2 * MODES :] = jnp.broadcast_to(dskip, (GROUP, c))
        for n in range(1, count):
            links.send(small_all.at[z], small_all.at[z], sm_s.at[n], sm_r.at[n], along(n))
        dq_own[...] = (dp[...] * field[...]).astype(bf16)
        dm = deinterleave(ys) + skip[...] * g
        dk_own[...] = (dm * val[...].astype(f32)).astype(bf16)
        dv_own[...] = (dm * key[...].astype(f32)).astype(bf16)
        for n, (src, dst) in enumerate([(dq_own, dq), (dk_own, dk), (dv_own, dv)]):
            copy = pltpu.make_async_copy(src, dst, loc.at[n])
            copy.start()
            done.append(copy)

    def out_near():
        for _ in rounds["w"]:
            pass
        got_one(WC.at[:, lanes(other, c)], 5)
        acc_ref[...] = out_part(0, near, None)

    def out_far():
        acc = out_part(near, CHIPS, acc_ref[...])
        out_all[mine, :] = jnp.where(is_first, acc[:, :c], acc[:, c:]).astype(bf16)
        out_send[...] = jnp.where(is_first, acc[:, c:], acc[:, :c]).astype(bf16)
        links.send(out_send, out_all.at[mine], one_s.at[6], one_r.at[6], mate)

    tasks = {
        "p0": product_near, "p1": product_far, "bs": back_states, "be": back_start,
        "b": back_piece, "bz": back_end, "o0": out_near, "o1": out_far,
    }
    for name in SCHEDULE:
        if name in tasks:
            tasks[name]()
        elif name[0] == "g":
            weight_part(int(name[1]))
        elif name[0] == "f":
            first.wave(int(name[1]))
        elif name[0] == "s":
            second.wave(int(name[1]))
        else:
            for one in name[1:]:
                next(rounds[one], None)
    for one in rounds.values():
        for _ in one:
            pass
    for n in range(1, count):
        here = small_all.at[ring.at(0, -n)]
        links.copy(here, here, sm_s.at[n], sm_r.at[n], mate).wait_recv()
    total = small_all[0]
    for n in range(1, count):
        total = total + small_all[n]
    small_sum[...] = total
    got_one(out_all.at[its], 6)
    for n, (src, dst) in enumerate([(small_sum, small), (out_all, out)]):
        copy = pltpu.make_async_copy(src, dst, loc.at[3 + n])
        copy.start()
        done.append(copy)
    links.drain()
    for copy in done:
        copy.wait()


def finish(out_in, dq_in, dk_in, dv_in, small, dw_in, out, dq, dk, dv, dres, drate, dskip, dw):
    out[...] = out_in[...]
    dq[...] = dq_in[...]
    dk[...] = dk_in[...]
    dv[...] = dv_in[...]
    dres[...] = small[:MODES]
    drate[...] = small[MODES : 2 * MODES]
    dskip[...] = small[2 * MODES : 2 * MODES + 1]
    dw[...] = dw_in[...].astype(f32)


def shards(queries, keys, values, residue, rate, skip, w_out, lengths, d_out):
    t, c = queries.shape
    n_out = w_out.shape[1]
    count = lax.axis_size("pos")
    thin = jax.ShapeDtypeStruct((t, c), bf16)
    rows = 2 * MODES + GROUP
    vmem, dma = pltpu.VMEM, pltpu.SemaphoreType.DMA
    wide, half, far = 2 * c, t // 2, count // 2
    tall, short = vmem((t, c), f32), vmem((t, c), bf16)
    few = vmem((MODES, c), f32)
    scratch = [
        short, short, short, few, few, vmem((1, c), f32), short, short, short,
        vmem((half, n_out), bf16), vmem((half, n_out), bf16), vmem((wide, n_out), bf16),
        vmem((CHIPS, wide, wide), bf16), tall, tall, tall,
        vmem((t // NSUB, MODES, NSUB, c), f32), tall, tall, vmem((half, c), f32),
        short, vmem((half, c), bf16), short,
        vmem((2, MODES, c), f32), vmem((2, 3, MODES, c), f32), vmem((count, rows, c), f32),
        vmem((rows, c), f32),
        vmem((c, n_out), f32), vmem((c, n_out), bf16), vmem((c, n_out), bf16),
        vmem((3, 2, 2, far + 1, c // count, 3 * wide), bf16), vmem((c, n_out), bf16),
        dma((2, len(KEYS))), dma((2, len(KEYS))), dma((2, len(KEYS))), dma((2, len(KEYS))),
        dma((9,)), dma((10,)), dma((10,)), dma((CHIPS,)), dma((CHIPS,)),
        dma((2, 2, far)), dma((2, 2, far)), dma((2, 3)), dma((2, 3)), dma((count,)), dma((count,)),
        dma((3, 2, 2, far)), dma((3, 2, 2, far)), dma((3, 2, 2, far)), dma((3, 2, 2, far)),
        vmem((half, wide), f32), dma((CHIPS,)),
    ]
    whole = pl.BlockSpec(memory_space=pltpu.VMEM)
    apart = pl.BlockSpec(memory_space=pl.ANY)
    out, dq, dk, dv, small, dw = pl.pallas_call(
        functools.partial(kernel, count),
        out_shape=(
            thin, thin, thin, thin, jax.ShapeDtypeStruct((rows, c), f32),
            jax.ShapeDtypeStruct((c, n_out), bf16),
        ),
        in_specs=[pl.BlockSpec(memory_space=pltpu.SMEM)] + [apart] * 8,
        out_specs=(apart,) * 6,
        scratch_shapes=scratch,
        compiler_params=pltpu.CompilerParams(
            collective_id=0, has_side_effects=True, vmem_limit_bytes=60 * MIB
        ),
    )(lengths, queries, keys, values, w_out, d_out, rate.T, residue.T, skip[None, :])
    state = jax.ShapeDtypeStruct((MODES, c), f32)
    out, dq, dk, dv, dres, drate, dskip, dw = pl.pallas_call(
        finish,
        out_shape=(
            thin, thin, thin, thin, state, state, jax.ShapeDtypeStruct((1, c), f32),
            jax.ShapeDtypeStruct((c, n_out), f32),
        ),
        in_specs=[whole] * 6,
        out_specs=(whole,) * 8,
        compiler_params=pltpu.CompilerParams(vmem_limit_bytes=60 * MIB),
    )(out, dq, dk, dv, small, dw)
    return out, dq, dk, dv, dres.T, drate.T, dskip[0], dw


def solution(mesh):
    both, chan = P("pos", "ch"), P("ch", None)
    return jax.shard_map(
        shards,
        mesh=mesh,
        in_specs=(both, both, both, chan, chan, P("ch"), chan, P(), both),
        out_specs=(both, both, both, both, chan, chan, P("ch"), chan),
        check_vma=False,
    )
```
